512 devices in a mesh: gx: 4 (over x), gy: 8 (over y, core), gz: 16 (over z).
Axes of the slice: x: 4, y: 4, z: 16, core: 2. Of those that a mesh axis runs over, the one named last changes fastest.
Arguments:
- volume: bfloat16 [2048, 512, 512], P('gz', 'gy', 'gx'), may hold values from -6 to 6
- tf_color: float32 [3, 16], replicated, may hold values from 0 to 1
- tf_opacity: float32 [16], replicated, may hold values from 0.0005 to 0.008
- active: int32 [256, 8, 4], P('gz', 'gy', 'gx'), may hold values from 0 to 1, as said below
Outputs:
- composited: float32 [4, 512, 768], P(None, ('gx', 'gy', 'gz'))
The draws below stay inside these ranges and needn't reach their ends.
Inputs may be any that keep to these rules, and one draw needn't show every extreme that they name: `active`: the 16 bricks of each block (one gy, gx index and 16 consecutive entries along the first dimension) hold at least one 1; in every draw some block has all 16 set.
All inputs are finite; a program needn't handle non-finite values.
Results may differ from the reference program's by a relative error of at most 0.0014.
Values may be sent and summed in bfloat16 or wider, within the bound.
No kernel may reach another device: no remote copies, remote signals or barrier semaphores. Data moves between devices by JAX's collectives and lax.ppermute only.
A program may use at most 64 MiB of HBM per device.

```python
import math
import jax
import jax.numpy as jnp
from jax import lax

CX = 128
CY = 64
CZ = 128
BZ = 8
KNOTS = 16
NX = 512
NY = 512
NZ = 2048
ZBRICKS = 256
IMAGE_COLS = 768
PIXELS = 393216
N_GX = 4
N_GY = 8
N_GZ = 16


def draw_active(key, part):
    key = jax.random.fold_in(key, 11)
    first, second, third, fourth = jax.random.split(key, 4)
    owners = (N_GZ, N_GY, N_GX)
    brick_count = CZ // BZ
    lower = jax.random.randint(first, owners, 1, brick_count + 1)
    upper = jax.random.randint(second, owners, 1, brick_count + 1)
    counts = jnp.minimum(lower, upper)
    chosen = jax.random.randint(third, (), 0, N_GZ * N_GY * N_GX)
    owner_ids = jnp.arange(N_GZ * N_GY * N_GX, dtype=jnp.int32).reshape(owners)
    counts = jnp.where(owner_ids == chosen, brick_count, counts)
    scores = jax.random.randint(fourth, owners + (brick_count,), 0, 2 ** 20) * brick_count + jnp.arange(brick_count, dtype=jnp.int32)
    ranks = jnp.argsort(jnp.argsort(scores, axis=-1), axis=-1)
    marks = (ranks < counts[..., None]).astype(jnp.int32)
    return jnp.transpose(marks, (0, 3, 1, 2)).reshape(ZBRICKS, N_GY, N_GX)


def levels(rng, extent, cuts, least, high):
    def one(axis_at, parts):
        steps = jax.random.uniform(jax.random.fold_in(jax.random.fold_in(rng, 6), axis_at), (parts,), jnp.float32, least / len(cuts), high / len(cuts))
        return jnp.repeat(jnp.exp(steps), extent[axis_at] // parts).reshape((-1,) + (1,) * (len(extent) - axis_at - 1))

    factor_of = one(*cuts[0])
    for cut in cuts[1:]:
        factor_of = factor_of * one(*cut)
    return factor_of


def bell_draw(rng, dims, spread, limit, cuts=(), held_as=jnp.bfloat16):
    result = spread * jax.random.normal(rng, dims, jnp.float32)
    if cuts:
        result = result * levels(rng, dims, cuts, -0.22, 0.18)
    return jnp.clip(result, -limit, limit).astype(held_as)


def setup_inputs(seed: int = 0) -> dict:
    key_list = jax.random.split(jax.random.key(seed), 5)
    return {
        "volume": bell_draw(key_list[0], (NZ, NY, NX), 1.0, 6.0, ((0, 16), (1, 8), (2, 4))),
        "tf_color": jnp.clip(jax.random.uniform(key_list[1], (3, KNOTS), jnp.float32, 0.0, 1.0), 0.0, 1.0),
        "tf_opacity": jnp.clip(jnp.exp(jax.random.uniform(key_list[2], (KNOTS,), jnp.float32, math.log(0.0005), math.log(0.008))), 0.0005, 0.008),
        "active": draw_active(jax.random.fold_in(key_list[4], 71), 0),
    }


LIMIT = 3.0


def classify(values, tf_color, tf_opacity):
    knot_count = tf_opacity.shape[0]
    spacing = 2.0 * LIMIT / (knot_count - 1)
    opacity = jnp.zeros(values.shape, jnp.float32)
    shades = [jnp.zeros(values.shape, jnp.float32) for channel in range(3)]
    for knot_index in range(knot_count):
        centre = -LIMIT + knot_index * spacing
        weight = jnp.maximum(0.0, 1.0 - jnp.abs(values - centre) / spacing)
        opacity = opacity + weight * tf_opacity[knot_index]
        shades = [shades[channel] + weight * tf_color[channel, knot_index] for channel in range(3)]
    return jnp.stack([shades[0] * opacity, shades[1] * opacity, shades[2] * opacity, opacity])


def composite(nearer, farther):
    return nearer + (1.0 - nearer[3:4]) * farther


def render_brick(cell_values, rim_cells, tf_color, tf_opacity):
    layers = cell_values.shape[0]
    classified = classify(cell_values.astype(jnp.float32), tf_color, tf_opacity)
    edge = classify(rim_cells.astype(jnp.float32), tf_color, tf_opacity)
    running = jnp.zeros((4,) + cell_values.shape[1:], jnp.float32)
    for layer_index in range(layers):
        fraction = layer_index / layers
        current = classified[:, layer_index]
        shifted = jnp.concatenate([edge[:, layer_index, :, None], current[:, :, :-1]], axis=2)
        sample = (1.0 - fraction) * current + fraction * shifted
        running = composite(running, sample)
    return running


def reference(volume, tf_color, tf_opacity, active):
    brick_count = CZ // BZ
    visits = jnp.array([(depth_block, col_block, row_block) for depth_block in range(N_GZ)
                        for col_block in reversed(range(N_GX)) for row_block in range(N_GY)], dtype=jnp.int32)
    picture = jnp.zeros((4, NY, IMAGE_COLS), jnp.float32)

    def advance(picture, visit):
        depth_block, col_block, row_block = visit[0], visit[1], visit[2]
        cells_block = lax.dynamic_slice(volume, (depth_block * CZ, row_block * CY, col_block * CX), (CZ, CY, CX))
        left_start = jnp.maximum(col_block * CX - 1, 0).astype(jnp.int32)
        column = lax.dynamic_slice(volume, (depth_block * CZ, row_block * CY, left_start), (CZ, CY, 1))[:, :, 0]
        column = jnp.where(col_block > 0, column, jnp.zeros_like(column))
        brick_marks = lax.dynamic_slice(active, (depth_block * brick_count, row_block, col_block), (brick_count, 1, 1)).reshape(brick_count)
        window = jnp.zeros((4, CY, CX + brick_count), jnp.float32)
        for brick_index in range(brick_count):
            image = render_brick(cells_block[brick_index * BZ:(brick_index + 1) * BZ],
                                 column[brick_index * BZ:(brick_index + 1) * BZ], tf_color, tf_opacity)
            image = image * brick_marks[brick_index].astype(jnp.float32)
            covered = window[:, :, brick_index:brick_index + CX]
            window = window.at[:, :, brick_index:brick_index + CX].set(composite(covered, image))
        corner = (jnp.int32(0), (row_block * CY).astype(jnp.int32), (col_block * CX + depth_block * brick_count).astype(jnp.int32))
        covered = lax.dynamic_slice(picture, corner, (4, CY, CX + brick_count))
        picture = lax.dynamic_update_slice(picture, composite(covered, window), corner)
        return picture, None

    picture, _ = lax.scan(advance, picture, visits)
    device_total = N_GX * N_GY * N_GZ
    flat_picture = picture.reshape(4, PIXELS // device_total, device_total)
    return jnp.transpose(flat_picture, (0, 2, 1))
```

```python
import functools

import jax
import jax.numpy as jnp
from jax import lax
from jax.experimental import pallas as pl
from jax.experimental.pallas import tpu as pltpu
from jax.sharding import PartitionSpec as P

BZ = 8
LIMIT = 3.0
KNOTS = 16
LANES = 128
GROUP = 16
STEPS = 4
F32 = jnp.float32


def lane_ids(rows):
    return lax.broadcasted_iota(jnp.int32, (rows, LANES), 1)


def pick(table, index):
    return jnp.take_along_axis(table, index, axis=1, mode="promise_in_bounds")


def build_tables(color_ref, opacity_ref, pad_ref, table_ref):
    pad_ref[...] = jnp.zeros_like(pad_ref)
    pad_ref[0:3, 0:KNOTS] = color_ref[...]
    pad_ref[3:4, 0:KNOTS] = opacity_ref[...]
    upper = pad_ref[...]
    lower = pltpu.roll(upper, 1, 1)
    slope = upper - lower
    base = lower - slope * lane_ids(8).astype(F32)
    for n in range(4):
        table_ref[n] = jnp.broadcast_to(base[n:n + 1], (GROUP, LANES))
        table_ref[4 + n] = jnp.broadcast_to(slope[n:n + 1], (GROUP, LANES))


def classify(values, tables):
    scale = (KNOTS - 1) / (2.0 * LIMIT)
    place = jnp.clip(values * scale + (LIMIT * scale + 1.0), 0.0, KNOTS + 1.0)
    index = place.astype(jnp.int32)
    return [pick(tables[n], index) + pick(tables[4 + n], index) * place for n in range(4)]


def render_kernel(flag_ref, color_ref, opacity_ref, volume_ref, front_ref, tail_ref,
                  pad_ref, table_ref, run_ref, done_ref):
    step = pl.program_id(0)
    rows_all = front_ref.shape[1]
    groups = rows_all // GROUP
    bricks = volume_ref.shape[0] // BZ

    @pl.when(step == 0)
    def _():
        build_tables(color_ref, opacity_ref, pad_ref, table_ref)
        for ref in (run_ref, done_ref):
            ref[0:3] = jnp.zeros((3, rows_all, LANES), F32)
            ref[3] = jnp.ones((rows_all, LANES), F32)

    lane = lane_ids(GROUP)

    def one(item, carry):
        local = item // groups
        brick = step * bricks + local
        rows = pl.ds(pl.multiple_of(item % groups * GROUP, GROUP), GROUP)
        tables = [table_ref[n] for n in range(8)]
        for k in range(BZ):
            f = k / BZ
            *shades, alpha = classify(volume_ref[local * BZ + k, rows, :].astype(F32), tables)
            if k == 0:
                here = [alpha * shade for shade in shades]
                clear = 1.0 - alpha
                continue
            moved = alpha * f
            kept = alpha - moved
            weight = clear * kept
            beside = pltpu.roll(clear, LANES - 1, 1) * moved
            here = [h + weight * shade for h, shade in zip(here, shades)]
            if k == 1:
                right = [beside * shade for shade in shades]
            else:
                right = [r + beside * shade for r, shade in zip(right, shades)]
            clear = clear - clear * (kept + pltpu.roll(moved, 1, 1))
        shown = jnp.where(lane == 0, 0.0, flag_ref[brick, 0, 0].astype(F32))
        image = [(h + pltpu.roll(r, 1, 1)) * shown for h, r in zip(here, right)]
        image.append((1.0 - clear) * shown)
        image = [pltpu.roll(value, brick, 1) for value in image]
        leaving = lane == brick - 1
        through = run_ref[3, rows, :]
        done_ref[3, rows, :] = jnp.where(leaving, through, done_ref[3, rows, :])
        through = jnp.where(leaving, 1.0, through)
        for n in range(3):
            sum_n = run_ref[n, rows, :]
            done_ref[n, rows, :] = jnp.where(leaving, sum_n, done_ref[n, rows, :])
            run_ref[n, rows, :] = jnp.where(leaving, 0.0, sum_n) + through * image[n]
        run_ref[3, rows, :] = through - through * image[3]
        return carry

    lax.fori_loop(0, bricks * groups, one, 0)

    @pl.when(step == pl.num_programs(0) - 1)
    def _():
        wide = lane_ids(rows_all)
        total = pl.num_programs(0) * bricks
        for n in range(4):
            last = run_ref[n] if n < 3 else 1.0 - run_ref[n]
            first = done_ref[n] if n < 3 else 1.0 - done_ref[n]
            front_ref[n] = jnp.where(wide < total - 1, first, last)
            tail_ref[n] = jnp.where(wide < total - 1, last, 0.0)


def render(active, tf_color, tf_opacity, volume):
    layers, rows, cols = volume.shape
    out = jax.ShapeDtypeStruct((4, rows, LANES), F32)
    whole = pl.BlockSpec((4, rows, LANES), lambda i: (0, 0, 0))
    return pl.pallas_call(
        render_kernel,
        grid=(STEPS,),
        in_specs=[
            pl.BlockSpec(memory_space=pltpu.SMEM),
            pl.BlockSpec(tf_color.shape, lambda i: (0, 0)),
            pl.BlockSpec(tf_opacity.shape, lambda i: (0, 0)),
            pl.BlockSpec((layers // STEPS, rows, cols), lambda i: (i, 0, 0)),
        ],
        out_specs=[whole, whole],
        out_shape=[out, out],
        scratch_shapes=[
            pltpu.VMEM((8, LANES), F32),
            pltpu.VMEM((8, GROUP, LANES), F32),
            pltpu.VMEM((4, rows, LANES), F32),
            pltpu.VMEM((4, rows, LANES), F32),
        ],
        cost_estimate=pl.CostEstimate(flops=40_000_000, bytes_accessed=2_400_000, transcendentals=0),
        compiler_params=pltpu.CompilerParams(vmem_limit_bytes=32 * 1024 * 1024),
        name="render",
    )(active, tf_color, tf_opacity, volume)


def deal_kernel(flag_ref, color_ref, opacity_ref, column_ref, rim_ref, front_ref, tail_ref, out_ref,
                pad_ref, table_ref, column_f32, rim_f32):
    build_tables(color_ref, opacity_ref, pad_ref, table_ref)
    tables = [table_ref[n] for n in range(8)]
    out_ref[...] = jnp.zeros_like(out_ref)
    total, rows = column_ref.shape
    bricks = total // BZ
    half = rows // 2
    column_f32[:, 0:rows] = column_ref[...].astype(F32)
    rim_f32[:, 0:rows] = rim_ref[...].astype(F32)
    start = lax.axis_index("gx") * LANES + lax.axis_index("gz") * bricks
    targets = out_ref.shape[0]
    lane = lane_ids(GROUP)
    flags = jnp.broadcast_to(flag_ref[...].astype(F32), (bricks, LANES))
    to_alpha = lane % half + 3 * half
    for parity in range(2):
        spread = lane % half * 2 + parity

        def shaded(ref, k):
            values = pick(ref[pl.ds(k, bricks, stride=BZ), :], spread)
            red, green, blue, alpha = classify(values, tables)
            shade = jnp.where(lane < half, red, jnp.where(lane < 2 * half, green, blue))
            return alpha * jnp.where(lane < 3 * half, shade, 1.0), alpha

        image = jnp.zeros((bricks, LANES), F32)
        clear = jnp.ones((bricks, LANES), F32)
        for k in range(BZ):
            f = k / BZ
            sample, alpha = shaded(column_f32, k)
            if k:
                beside, beside_alpha = shaded(rim_f32, k)
                sample = (1.0 - f) * sample + f * beside
                alpha = (1.0 - f) * alpha + f * beside_alpha
            image = image + clear * sample
            clear = clear - clear * alpha
        image = image * flags
        near = jnp.concatenate([front_ref[n, pl.ds(parity, half, stride=2), :] for n in range(4)], axis=0).T
        far = jnp.concatenate([tail_ref[n, pl.ds(parity, half, stride=2), :] for n in range(4)], axis=0).T
        for m in range(LANES // GROUP + 1):
            place = lax.rem(start + parity * (targets // 2) + m * GROUP, targets)
            piece = near[m * GROUP:(m + 1) * GROUP] if m < LANES // GROUP else far[:GROUP]
            if m == 0:
                piece = piece + (1.0 - pick(piece, to_alpha)) * image
            out_ref[pl.ds(pl.multiple_of(place, GROUP), GROUP), :] = piece


def deal(active, tf_color, tf_opacity, column, rim, front, tail, targets):
    return pl.pallas_call(
        deal_kernel,
        out_shape=jax.ShapeDtypeStruct((targets, LANES), F32),
        scratch_shapes=[
            pltpu.VMEM((8, LANES), F32),
            pltpu.VMEM((8, GROUP, LANES), F32),
            pltpu.VMEM((column.shape[0], LANES), F32),
            pltpu.VMEM((column.shape[0], LANES), F32),
        ],
        compiler_params=pltpu.CompilerParams(vmem_limit_bytes=32 * 1024 * 1024),
        name="deal",
    )(active, tf_color, tf_opacity, column, rim, front, tail)


def gather_kernel(across, down, depth, bricks, arrived_ref, out_ref):
    targets = across * down * depth
    me = (lax.axis_index("gx") * down + lax.axis_index("gy")) * depth + lax.axis_index("gz")
    half = LANES // 4
    lane = lane_ids(down)
    to_alpha = lane % half + 3 * half
    total = [jnp.zeros((down, LANES), F32) for k in range(3)]
    clear = [jnp.ones((down, LANES), F32) for k in range(3)]
    for front in range(depth):
        for x in reversed(range(across)):
            start = x * LANES + front * bricks
            behind = lax.rem(me - start + 2 * targets, targets)
            slot = jnp.where(me < start, 1, 0) + jnp.where(behind >= targets // 2, 1, 0)
            piece = arrived_ref[pl.ds(x * down * depth + front, down, stride=depth), :]
            alpha = pick(piece, to_alpha)
            for k in range(3):
                mine = jnp.where(slot == k, 1.0, 0.0)
                total[k] = total[k] + clear[k] * (piece * mine)
                clear[k] = clear[k] - clear[k] * (alpha * mine)
    width = 3 * half
    third = lane % 3
    for c in range(4):
        source = jnp.minimum(lane // 3, half - 1) + c * half
        spread = [pick(value, source) for value in total]
        row = jnp.where(third == 0, spread[0], jnp.where(third == 1, spread[1], spread[2]))
        for y in range(down):
            out_ref[c, 0:1, y * width:(y + 1) * width] = row[y:y + 1, 0:width]


def gather(arrived, across, down, depth, bricks):
    pixels = down * 3 * LANES // 4
    return pl.pallas_call(
        functools.partial(gather_kernel, across, down, depth, bricks),
        out_shape=jax.ShapeDtypeStruct((4, 1, pixels), F32),
        compiler_params=pltpu.CompilerParams(vmem_limit_bytes=32 * 1024 * 1024),
        name="gather",
    )(arrived)


def body(volume, tf_color, tf_opacity, active):
    layers = volume.shape[0]
    bricks = layers // BZ
    across, down, depth = (lax.axis_size(name) for name in ("gx", "gy", "gz"))
    targets = across * down * depth
    opacity = tf_opacity.reshape(1, -1)
    rim = lax.ppermute(volume[:, :, -1], "gx", [(i, i + 1) for i in range(across - 1)])
    column = volume[:, :, 0]
    front, tail = render(active, tf_color, opacity, volume)
    rows = deal(active.reshape(bricks, 1), tf_color, opacity, column, rim, front, tail, targets)
    arrived = lax.all_to_all(rows, ("gx", "gy", "gz"), 0, 0, tiled=True)
    return gather(arrived, across, down, depth, bricks)


def solution(mesh):
    placed = (P("gz", "gy", "gx"), P(), P(), P("gz", "gy", "gx"))
    return jax.shard_map(
        body,
        mesh=mesh,
        in_specs=placed,
        out_specs=P(None, ("gx", "gy", "gz"), None),
        check_vma=False,
    )
```

```python
import functools

import jax
import jax.numpy as jnp
from jax import lax
from jax.experimental import pallas as pl
from jax.experimental.pallas import tpu as pltpu
from jax.sharding import PartitionSpec as P

BZ = 8
LIMIT = 3.0
KNOTS = 16
LANES = 128
GROUP = 16
STEPS = 4
UNROLL = 4
CHAINED = (2, 5)
F32 = jnp.float32


def lane_ids(rows):
    return lax.broadcasted_iota(jnp.int32, (rows, LANES), 1)


def pick(table, index):
    return jnp.take_along_axis(table, index, axis=1, mode="promise_in_bounds")


def build_tables(color_ref, opacity_ref, pad_ref, table_ref):
    pad_ref[...] = jnp.zeros_like(pad_ref)
    pad_ref[0:3, 0:KNOTS] = color_ref[...]
    pad_ref[3:4, 0:KNOTS] = opacity_ref[...]
    upper = pad_ref[...]
    lower = pltpu.roll(upper, 1, 1)
    slope = upper - lower
    base = lower - slope * lane_ids(8).astype(F32)
    for n in range(4):
        table_ref[n] = jnp.broadcast_to(base[n:n + 1], (GROUP, LANES))
        table_ref[4 + n] = jnp.broadcast_to(slope[n:n + 1], (GROUP, LANES))


def classify(values, tables):
    scale = (KNOTS - 1) / (2.0 * LIMIT)
    place = jnp.clip(values * scale + (LIMIT * scale + 1.0), 0.0, KNOTS + 1.0)
    index = place.astype(jnp.int32)
    got = [pick(table, index) for table in tables]
    return [got[n] + got[4 + n] * place for n in range(4)]


def climb(values, knot_ref):
    scale = (KNOTS - 1) / (2.0 * LIMIT)
    place = values * scale + (LIMIT * scale + 1.0)
    base = [jnp.zeros_like(values) for n in range(4)]
    slope = [knot_ref[4 + n, 0] for n in range(4)]
    for k in range(KNOTS + 2):
        above = place >= float(k)
        for n in range(4):
            if k:
                base[n] = jnp.where(above, knot_ref[n, k], base[n])
            slope[n] = jnp.where(above, knot_ref[4 + n, k], slope[n] if k else 0.0)
    return [base[n] + slope[n] * place for n in range(4)]


def render_kernel(flag_ref, color_ref, opacity_ref, volume_ref, front_ref, tail_ref,
                  pad_ref, table_ref, run_ref, done_ref, seen_ref, knot_ref):
    step = pl.program_id(0)
    rows_all = front_ref.shape[1]
    groups = rows_all // GROUP
    bricks = volume_ref.shape[0] // BZ

    @pl.when(step == 0)
    def _():
        build_tables(color_ref, opacity_ref, pad_ref, table_ref)
        for n in range(8):
            for k in range(KNOTS + 2):
                knot_ref[n, k] = pick(table_ref[n, 0:8], jnp.full((8, LANES), k, jnp.int32))
        for ref in (run_ref, done_ref):
            ref[0:3] = jnp.zeros((3, rows_all, LANES), F32)
            ref[3] = jnp.ones((rows_all, LANES), F32)

    lane = lane_ids(GROUP)
    layers = volume_ref.shape[0]

    def look(layer, carry):
        tables = [table_ref[n, 0:8] for n in range(8)]
        for start in range(0, rows_all, GROUP):
            pair = volume_ref[layer, start:start + GROUP, :].astype(F32)
            for q in range(0, GROUP, 8):
                at = start + q
                if at // 8 in CHAINED:
                    found = climb(pair[q:q + 8], knot_ref)
                else:
                    found = classify(pair[q:q + 8], tables)
                for n in range(4):
                    seen_ref[n, layer, at:at + 8, :] = found[n]
        return carry

    lax.fori_loop(0, layers, look, 0, unroll=UNROLL)

    def one(local, carry):
        brick = step * bricks + local
        for group in range(groups):
            rows = slice(group * GROUP, (group + 1) * GROUP)
            for k in range(BZ):
                f = k / BZ
                *shades, alpha = [seen_ref[n, local * BZ + k, rows, :] for n in range(4)]
                if k == 0:
                    here = [alpha * shade for shade in shades]
                    clear = 1.0 - alpha
                    continue
                moved = alpha * f
                kept = alpha - moved
                weight = clear * kept
                beside = pltpu.roll(clear, LANES - 1, 1) * moved
                here = [h + weight * shade for h, shade in zip(here, shades)]
                if k == 1:
                    right = [beside * shade for shade in shades]
                else:
                    right = [r + beside * shade for r, shade in zip(right, shades)]
                clear = clear - clear * (kept + pltpu.roll(moved, 1, 1))
            flag = flag_ref[brick].astype(F32)
            shown = jnp.where(lane == 0, 0.0, flag)
            passed = jnp.where(lane == LANES - 1, 0.0, flag)
            image = [pltpu.roll(h * shown, brick, 1) + pltpu.roll(r * passed, brick + 1, 1)
                     for h, r in zip(here, right)]
            image.append(pltpu.roll((1.0 - clear) * shown, brick, 1))
            leaving = lane == brick - 1
            through = run_ref[3, rows, :]
            done_ref[3, rows, :] = jnp.where(leaving, through, done_ref[3, rows, :])
            through = jnp.where(leaving, 1.0, through)
            for n in range(3):
                sum_n = run_ref[n, rows, :]
                done_ref[n, rows, :] = jnp.where(leaving, sum_n, done_ref[n, rows, :])
                run_ref[n, rows, :] = jnp.where(leaving, 0.0, sum_n) + through * image[n]
            run_ref[3, rows, :] = through - through * image[3]
        return carry

    lax.fori_loop(0, bricks, one, 0)

    @pl.when(step == pl.num_programs(0) - 1)
    def _():
        wide = lane_ids(rows_all)
        total = pl.num_programs(0) * bricks
        for n in range(4):
            last = run_ref[n] if n < 3 else 1.0 - run_ref[n]
            first = done_ref[n] if n < 3 else 1.0 - done_ref[n]
            front_ref[n] = jnp.where(wide < total - 1, first, last)
            tail_ref[n] = jnp.where(wide < total - 1, last, 0.0)


def render(active, tf_color, tf_opacity, volume):
    layers, rows, cols = volume.shape
    out = jax.ShapeDtypeStruct((4, rows, LANES), F32)
    whole = pl.BlockSpec((4, rows, LANES), lambda i: (0, 0, 0))
    return pl.pallas_call(
        render_kernel,
        grid=(STEPS,),
        in_specs=[
            pl.BlockSpec(memory_space=pltpu.SMEM),
            pl.BlockSpec(tf_color.shape, lambda i: (0, 0)),
            pl.BlockSpec(tf_opacity.shape, lambda i: (0, 0)),
            pl.BlockSpec((layers // STEPS, rows, cols), lambda i: (i, 0, 0)),
        ],
        out_specs=[whole, whole],
        out_shape=[out, out],
        scratch_shapes=[
            pltpu.VMEM((8, LANES), F32),
            pltpu.VMEM((8, GROUP, LANES), F32),
            pltpu.VMEM((4, rows, LANES), F32),
            pltpu.VMEM((4, rows, LANES), F32),
            pltpu.VMEM((4, layers // STEPS, rows, LANES), F32),
            pltpu.VMEM((8, KNOTS + 2, 8, LANES), F32),
        ],
        cost_estimate=pl.CostEstimate(flops=40_000_000, bytes_accessed=2_400_000, transcendentals=0),
        compiler_params=pltpu.CompilerParams(vmem_limit_bytes=32 * 1024 * 1024),
        name="render",
    )(active, tf_color, tf_opacity, volume)


def deal_kernel(flag_ref, color_ref, opacity_ref, column_ref, rim_ref, front_ref, tail_ref, out_ref,
                pad_ref, table_ref):
    build_tables(color_ref, opacity_ref, pad_ref, table_ref)
    tables = [table_ref[n] for n in range(8)]
    out_ref[...] = jnp.zeros_like(out_ref)
    rows = front_ref.shape[1]
    beside = LANES // rows
    bricks = column_ref.shape[0] * beside // BZ
    half = rows // 2
    start = lax.axis_index("gx") * LANES + lax.axis_index("gz") * bricks
    targets = out_ref.shape[0]
    lane = lane_ids(GROUP)
    deep = lax.broadcasted_iota(jnp.int32, (bricks, LANES), 0)
    flags = jnp.zeros((bricks, LANES), F32)
    for b in range(bricks):
        flags = jnp.where(deep == b, flag_ref[b].astype(F32), flags)
    to_alpha = lane % half + 3 * half
    for parity in range(2):
        spread = lane % half * 2 + parity

        def shaded(ref, k):
            values = pick(ref[pl.ds(k // beside, bricks, stride=BZ // beside), :], spread + k % beside * rows)
            red, green, blue, alpha = classify(values, tables)
            shade = jnp.where(lane < half, red, jnp.where(lane < 2 * half, green, blue))
            return alpha * jnp.where(lane < 3 * half, shade, 1.0), alpha

        image = jnp.zeros((bricks, LANES), F32)
        clear = jnp.ones((bricks, LANES), F32)
        for k in range(BZ):
            f = k / BZ
            sample, alpha = shaded(column_ref, k)
            if k:
                left, left_alpha = shaded(rim_ref, k)
                sample = (1.0 - f) * sample + f * left
                alpha = (1.0 - f) * alpha + f * left_alpha
            image = image + clear * sample
            clear = clear - clear * alpha
        image = image * flags
        near = jnp.concatenate([front_ref[n, pl.ds(parity, half, stride=2), :] for n in range(4)], axis=0).T
        far = jnp.concatenate([tail_ref[n, pl.ds(parity, half, stride=2), :] for n in range(4)], axis=0).T
        for m in range(LANES // GROUP + 1):
            place = lax.rem(start + parity * (targets // 2) + m * GROUP, targets)
            piece = near[m * GROUP:(m + 1) * GROUP] if m < LANES // GROUP else far[:GROUP]
            if m == 0:
                piece = piece + (1.0 - pick(piece, to_alpha)) * image
            out_ref[pl.ds(pl.multiple_of(place, GROUP), GROUP), :] = piece


def deal(active, tf_color, tf_opacity, column, rim, front, tail, targets):
    vmem = pl.BlockSpec(memory_space=pltpu.VMEM)
    return pl.pallas_call(
        deal_kernel,
        in_specs=[pl.BlockSpec(memory_space=pltpu.SMEM)] + [vmem] * 6,
        out_specs=vmem,
        out_shape=jax.ShapeDtypeStruct((targets, LANES), F32),
        scratch_shapes=[
            pltpu.VMEM((8, LANES), F32),
            pltpu.VMEM((8, GROUP, LANES), F32),
        ],
        compiler_params=pltpu.CompilerParams(vmem_limit_bytes=32 * 1024 * 1024),
        name="deal",
    )(active, tf_color, tf_opacity, column, rim, front, tail)


def gather_kernel(across, down, depth, bricks, arrived_ref, out_ref):
    targets = across * down * depth
    me = (lax.axis_index("gx") * down + lax.axis_index("gy")) * depth + lax.axis_index("gz")
    half = LANES // 4
    lane = lane_ids(down)
    to_alpha = lane % half + 3 * half
    total = [jnp.zeros((down, LANES), F32) for k in range(3)]
    clear = [jnp.ones((down, LANES), F32) for k in range(3)]
    for front in range(depth):
        for x in reversed(range(across)):
            start = x * LANES + front * bricks
            behind = lax.rem(me - start + 2 * targets, targets)
            slot = jnp.where(me < start, 1, 0) + jnp.where(behind >= targets // 2, 1, 0)
            piece = arrived_ref[pl.ds(x * down * depth + front, down, stride=depth), :]
            alpha = pick(piece, to_alpha)
            for k in range(3):
                mine = jnp.where(slot == k, 1.0, 0.0)
                total[k] = total[k] + clear[k] * (piece * mine)
                clear[k] = clear[k] - clear[k] * (alpha * mine)
    width = 3 * half
    third = lane % 3
    for c in range(4):
        source = jnp.minimum(lane // 3, half - 1) + c * half
        spread = [pick(value, source) for value in total]
        row = jnp.where(third == 0, spread[0], jnp.where(third == 1, spread[1], spread[2]))
        for y in range(down):
            out_ref[c, 0:1, y * width:(y + 1) * width] = row[y:y + 1, 0:width]


def gather(arrived, across, down, depth, bricks):
    pixels = down * 3 * LANES // 4
    return pl.pallas_call(
        functools.partial(gather_kernel, across, down, depth, bricks),
        out_shape=jax.ShapeDtypeStruct((4, 1, pixels), F32),
        compiler_params=pltpu.CompilerParams(vmem_limit_bytes=32 * 1024 * 1024),
        name="gather",
    )(arrived)


def ends_kernel(volume_ref, first_ref, last_ref):
    layers, rows, cols = volume_ref.shape
    part = 16
    row = lax.broadcasted_iota(jnp.int32, (16, cols), 0)
    lane = lax.broadcasted_iota(jnp.int32, (16, cols), 1)
    unit = jnp.where(lane == jnp.where(row == 0, 0, cols - 1), 1.0, 0.0).astype(jnp.bfloat16)
    for start in range(0, layers, part):
        cells = volume_ref[start:start + part].reshape(part * rows, cols)
        both = lax.dot_general(unit, cells, (((1,), (1,)), ((), ())), preferred_element_type=F32)
        first_ref[:, start * rows:(start + part) * rows] = both[0:1]
        last_ref[:, start * rows:(start + part) * rows] = both[1:2]


def ends(volume):
    layers, rows, cols = volume.shape
    out = jax.ShapeDtypeStruct((1, layers * rows), F32)
    first, last = pl.pallas_call(
        ends_kernel,
        out_shape=[out, out],
        compiler_params=pltpu.CompilerParams(vmem_limit_bytes=32 * 1024 * 1024),
        name="ends",
    )(volume)
    return first.reshape(-1, LANES), last.reshape(-1, LANES)


def body(volume, tf_color, tf_opacity, active):
    layers = volume.shape[0]
    bricks = layers // BZ
    across, down, depth = (lax.axis_size(name) for name in ("gx", "gy", "gz"))
    targets = across * down * depth
    opacity = tf_opacity.reshape(1, -1)
    flags = active.reshape(bricks)
    column, last = ends(volume)
    rim = lax.ppermute(last, "gx", [(i, i + 1) for i in range(across - 1)])
    front, tail = render(flags, tf_color, opacity, volume)
    rows = deal(flags, tf_color, opacity, column, rim, front, tail, targets)
    arrived = lax.all_to_all(rows, ("gx", "gy", "gz"), 0, 0, tiled=True)
    return gather(arrived, across, down, depth, bricks)


def solution(mesh):
    placed = (P("gz", "gy", "gx"), P(), P(), P("gz", "gy", "gx"))
    return jax.shard_map(
        body,
        mesh=mesh,
        in_specs=placed,
        out_specs=P(None, ("gx", "gy", "gz"), None),
        check_vma=False,
    )
```

```python
import functools

import jax
import jax.numpy as jnp
from jax import lax
from jax.experimental import pallas as pl
from jax.experimental.pallas import tpu as pltpu
from jax.sharding import PartitionSpec as P

BZ = 8
LIMIT = 3.0
KNOTS = 16
LANES = 128
GROUP = 16
STEPS = 4
UNROLL = 4
CHAINED = (2, 5)
F32 = jnp.float32


def lane_ids(rows):
    return lax.broadcasted_iota(jnp.int32, (rows, LANES), 1)


def pick(table, index):
    return jnp.take_along_axis(table, index, axis=1, mode="promise_in_bounds")


def build_tables(color_ref, opacity_ref, pad_ref, table_ref):
    pad_ref[...] = jnp.zeros_like(pad_ref)
    pad_ref[0:3, 0:KNOTS] = color_ref[...]
    pad_ref[3:4, 0:KNOTS] = opacity_ref[...]
    upper = pad_ref[...]
    lower = pltpu.roll(upper, 1, 1)
    slope = upper - lower
    base = lower - slope * lane_ids(8).astype(F32)
    for n in range(4):
        table_ref[n] = jnp.broadcast_to(base[n:n + 1], (GROUP, LANES))
        table_ref[4 + n] = jnp.broadcast_to(slope[n:n + 1], (GROUP, LANES))


def classify(values, tables):
    scale = (KNOTS - 1) / (2.0 * LIMIT)
    place = jnp.clip(values * scale + (LIMIT * scale + 1.0), 0.0, KNOTS + 1.0)
    index = place.astype(jnp.int32)
    got = [pick(table, index) for table in tables]
    return [got[n] + got[4 + n] * place for n in range(4)]


def climb(values, knot_ref):
    scale = (KNOTS - 1) / (2.0 * LIMIT)
    place = values * scale + (LIMIT * scale + 1.0)
    base = [jnp.zeros_like(values) for n in range(4)]
    slope = [knot_ref[4 + n, 0] for n in range(4)]
    for k in range(KNOTS + 2):
        above = place >= float(k)
        for n in range(4):
            if k:
                base[n] = jnp.where(above, knot_ref[n, k], base[n])
            slope[n] = jnp.where(above, knot_ref[4 + n, k], slope[n] if k else 0.0)
    return [base[n] + slope[n] * place for n in range(4)]


def render_kernel(flag_ref, color_ref, opacity_ref, volume_ref, front_ref, tail_ref,
                  pad_ref, table_ref, run_ref, done_ref, seen_ref, knot_ref):
    step = pl.program_id(0)
    rows_all = front_ref.shape[1]
    groups = rows_all // GROUP
    bricks = volume_ref.shape[0] // BZ

    @pl.when(step == 0)
    def _():
        build_tables(color_ref, opacity_ref, pad_ref, table_ref)
        for n in range(8):
            for k in range(KNOTS + 2):
                knot_ref[n, k] = pick(table_ref[n, 0:8], jnp.full((8, LANES), k, jnp.int32))
        for ref in (run_ref, done_ref):
            ref[0:3] = jnp.zeros((3, rows_all, LANES), F32)
            ref[3] = jnp.ones((rows_all, LANES), F32)

    lane = lane_ids(GROUP)
    layers = volume_ref.shape[0]

    def look(layer, carry):
        tables = [table_ref[n, 0:8] for n in range(8)]
        for start in range(0, rows_all, GROUP):
            pair = volume_ref[layer, start:start + GROUP, :].astype(F32)
            for q in range(0, GROUP, 8):
                at = start + q
                if at // 8 in CHAINED:
                    found = climb(pair[q:q + 8], knot_ref)
                else:
                    found = classify(pair[q:q + 8], tables)
                for n in range(4):
                    seen_ref[n, layer, at:at + 8, :] = found[n]
        return carry

    lax.fori_loop(0, layers, look, 0, unroll=UNROLL)

    def one(local, carry):
        brick = step * bricks + local
        for group in range(groups):
            rows = slice(group * GROUP, (group + 1) * GROUP)
            for k in range(BZ):
                f = k / BZ
                *shades, alpha = [seen_ref[n, local * BZ + k, rows, :] for n in range(4)]
                if k == 0:
                    here = [alpha * shade for shade in shades]
                    clear = 1.0 - alpha
                    continue
                moved = alpha * f
                kept = alpha - moved
                weight = clear * kept
                beside = pltpu.roll(clear, LANES - 1, 1) * moved
                here = [h + weight * shade for h, shade in zip(here, shades)]
                if k == 1:
                    right = [beside * shade for shade in shades]
                else:
                    right = [r + beside * shade for r, shade in zip(right, shades)]
                clear = clear - clear * (kept + pltpu.roll(moved, 1, 1))
            flag = flag_ref[brick].astype(F32)
            shown = jnp.where(lane == 0, 0.0, flag)
            passed = jnp.where(lane == LANES - 1, 0.0, flag)
            image = [pltpu.roll(h * shown, brick, 1) + pltpu.roll(r * passed, brick + 1, 1)
                     for h, r in zip(here, right)]
            image.append(pltpu.roll((1.0 - clear) * shown, brick, 1))
            leaving = lane == brick - 1
            through = run_ref[3, rows, :]
            done_ref[3, rows, :] = jnp.where(leaving, through, done_ref[3, rows, :])
            through = jnp.where(leaving, 1.0, through)
            for n in range(3):
                sum_n = run_ref[n, rows, :]
                done_ref[n, rows, :] = jnp.where(leaving, sum_n, done_ref[n, rows, :])
                run_ref[n, rows, :] = jnp.where(leaving, 0.0, sum_n) + through * image[n]
            run_ref[3, rows, :] = through - through * image[3]
        return carry

    lax.fori_loop(0, bricks, one, 0)

    @pl.when(step == pl.num_programs(0) - 1)
    def _():
        wide = lane_ids(rows_all)
        total = pl.num_programs(0) * bricks
        for n in range(4):
            last = run_ref[n] if n < 3 else 1.0 - run_ref[n]
            first = done_ref[n] if n < 3 else 1.0 - done_ref[n]
            front_ref[n] = jnp.where(wide < total - 1, first, last)
            tail_ref[n] = jnp.where(wide < total - 1, last, 0.0)


def render(active, tf_color, tf_opacity, volume):
    layers, rows, cols = volume.shape
    out = jax.ShapeDtypeStruct((4, rows, LANES), F32)
    whole = pl.BlockSpec((4, rows, LANES), lambda i: (0, 0, 0))
    return pl.pallas_call(
        render_kernel,
        grid=(STEPS,),
        in_specs=[
            pl.BlockSpec(memory_space=pltpu.SMEM),
            pl.BlockSpec(tf_color.shape, lambda i: (0, 0)),
            pl.BlockSpec(tf_opacity.shape, lambda i: (0, 0)),
            pl.BlockSpec((layers // STEPS, rows, cols), lambda i: (i, 0, 0)),
        ],
        out_specs=[whole, whole],
        out_shape=[out, out],
        scratch_shapes=[
            pltpu.VMEM((8, LANES), F32),
            pltpu.VMEM((8, GROUP, LANES), F32),
            pltpu.VMEM((4, rows, LANES), F32),
            pltpu.VMEM((4, rows, LANES), F32),
            pltpu.VMEM((4, layers // STEPS, rows, LANES), F32),
            pltpu.VMEM((8, KNOTS + 2, 8, LANES), F32),
        ],
        cost_estimate=pl.CostEstimate(flops=40_000_000, bytes_accessed=2_400_000, transcendentals=0),
        compiler_params=pltpu.CompilerParams(vmem_limit_bytes=32 * 1024 * 1024),
        name="render",
    )(active, tf_color, tf_opacity, volume)


def rim_image(column_ref, rim_ref, flag_ref, tables, rows):
    pairs = BZ * rows // LANES
    bricks = column_ref.shape[0] // pairs
    lane = lane_ids(bricks)
    second = lane >= rows
    deep = lax.broadcasted_iota(jnp.int32, (bricks, LANES), 0)
    flags = jnp.zeros((bricks, LANES), F32)
    for b in range(bricks):
        flags = jnp.where(deep == b, flag_ref[b].astype(F32), flags)
    image = [jnp.zeros((bricks, LANES), F32) for c in range(4)]
    clear = jnp.ones((bricks, LANES), F32)
    for pair in range(pairs):
        f = jnp.where(second, (2 * pair + 1) / BZ, 2 * pair / BZ)
        *own, alpha = classify(column_ref[pl.ds(pair, bricks, stride=pairs), :], tables)
        *left, beside = classify(rim_ref[pl.ds(pair, bricks, stride=pairs), :], tables)
        kept = (1.0 - f) * alpha
        moved = f * beside
        sample = [kept * a + moved * b for a, b in zip(own, left)] + [kept + moved]
        for part in (sample, [pltpu.roll(value, rows, 1) for value in sample]):
            image = [total + clear * value for total, value in zip(image, part)]
            clear = clear - clear * part[3]
    return [value * flags for value in image]


def deal_kernel(flag_ref, color_ref, opacity_ref, column_ref, rim_ref, front_ref, tail_ref, out_ref,
                pad_ref, table_ref):
    build_tables(color_ref, opacity_ref, pad_ref, table_ref)
    tables = [table_ref[n] for n in range(8)]
    rows = front_ref.shape[1]
    half = rows // 2
    lane = lane_ids(GROUP)
    to_alpha = lane % half + 3 * half
    rim = rim_image(column_ref, rim_ref, flag_ref, tables, rows)
    pieces = LANES // GROUP + 1
    for parity in range(2):
        spread = [pick(value, lane % half * 2 + parity) for value in rim]
        image = jnp.where(lane < half, spread[0], jnp.where(
            lane < 2 * half, spread[1], jnp.where(lane < 3 * half, spread[2], spread[3])))
        near = jnp.concatenate([front_ref[n, pl.ds(parity, half, stride=2), :] for n in range(4)], axis=0).T
        far = jnp.concatenate([tail_ref[n, pl.ds(parity, half, stride=2), :] for n in range(4)], axis=0).T
        for m in range(pieces):
            piece = near[m * GROUP:(m + 1) * GROUP] if m < pieces - 1 else far[:GROUP]
            if m == 0:
                piece = piece + (1.0 - pick(piece, to_alpha)) * image
            out_ref[pl.ds(m * 2 + parity, GROUP, stride=2 * pieces), :] = piece


def deal(flags, tf_color, tf_opacity, column, rim, front, tail):
    vmem = pl.BlockSpec(memory_space=pltpu.VMEM)
    return pl.pallas_call(
        deal_kernel,
        in_specs=[pl.BlockSpec(memory_space=pltpu.SMEM)] + [vmem] * 6,
        out_specs=vmem,
        out_shape=jax.ShapeDtypeStruct((2 * (LANES + GROUP), LANES), F32),
        scratch_shapes=[
            pltpu.VMEM((8, LANES), F32),
            pltpu.VMEM((8, GROUP, LANES), F32),
        ],
        compiler_params=pltpu.CompilerParams(vmem_limit_bytes=32 * 1024 * 1024),
        name="deal",
    )(flags, tf_color, tf_opacity, column, rim, front, tail)


def along_depth_kernel(across, down, depth, arrived_ref, out_ref, total_ref, clear_ref):
    taken = arrived_ref.shape[0] // depth
    total_ref[...] = jnp.zeros_like(total_ref)
    clear_ref[...] = jnp.ones_like(clear_ref)
    quarter = LANES // 4
    lane = lane_ids(taken)
    to_alpha = lane % quarter + 3 * quarter
    for z in range(depth):
        piece = arrived_ref[z * taken:(z + 1) * taken, :]
        alpha = pick(piece, to_alpha)
        place = slice(2 * z, 2 * z + taken)
        clear = clear_ref[place, :]
        total_ref[place, :] = total_ref[place, :] + clear * piece
        clear_ref[place, :] = clear - clear * alpha
    span = 2 * down
    even = lax.broadcasted_iota(jnp.int32, (span, LANES), 0) % 2 == 0
    blocks = [total_ref[q * span:(q + 1) * span, :] for q in range(3)]
    blocks.append(jnp.zeros((span, LANES), F32))
    x = lax.axis_index("gx")
    for q in range(across):
        place = lax.rem(x + q, across) * span
        out_ref[pl.ds(pl.multiple_of(place, span), span), :] = jnp.where(even, blocks[q], blocks[(q + 2) % 4])


def along_depth(arrived, across, down, depth):
    return pl.pallas_call(
        functools.partial(along_depth_kernel, across, down, depth),
        out_shape=jax.ShapeDtypeStruct((across * down * 2, LANES), F32),
        scratch_shapes=[pltpu.VMEM((6 * down, LANES), F32), pltpu.VMEM((6 * down, LANES), F32)],
        compiler_params=pltpu.CompilerParams(vmem_limit_bytes=32 * 1024 * 1024),
        name="along_depth",
    )(arrived)


def gather_kernel(across, down, arrived_ref, out_ref):
    me = lax.axis_index("gx")
    half = LANES // 4
    lane = lane_ids(down)
    to_alpha = lane % half + 3 * half
    total = [jnp.zeros((down, LANES), F32) for k in range(3)]
    clear = [jnp.ones((down, LANES), F32) for k in range(3)]
    for x in reversed(range(across)):
        slots = (jnp.where(me < x, 1, 0), jnp.where(me >= x + 2, 1, 2))
        for parity in range(2):
            piece = arrived_ref[pl.ds(x * 2 * down + parity, down, stride=2), :]
            alpha = pick(piece, to_alpha)
            for k in range(2) if parity == 0 else range(1, 3):
                mine = jnp.where(slots[parity] == k, 1.0, 0.0)
                total[k] = total[k] + clear[k] * (piece * mine)
                clear[k] = clear[k] - clear[k] * (alpha * mine)
    width = 3 * half
    third = lane % 3
    for c in range(4):
        source = jnp.minimum(lane // 3, half - 1) + c * half
        spread = [pick(value, source) for value in total]
        row = jnp.where(third == 0, spread[0], jnp.where(third == 1, spread[1], spread[2]))
        for y in range(down):
            out_ref[c, 0:1, y * width:(y + 1) * width] = row[y:y + 1, 0:width]


def gather(arrived, across, down):
    pixels = down * 3 * LANES // 4
    return pl.pallas_call(
        functools.partial(gather_kernel, across, down),
        out_shape=jax.ShapeDtypeStruct((4, 1, pixels), F32),
        compiler_params=pltpu.CompilerParams(vmem_limit_bytes=32 * 1024 * 1024),
        name="gather",
    )(arrived)


def ends_kernel(volume_ref, first_ref, last_ref):
    layers, rows, cols = volume_ref.shape
    part = 16
    row = lax.broadcasted_iota(jnp.int32, (16, cols), 0)
    lane = lax.broadcasted_iota(jnp.int32, (16, cols), 1)
    unit = jnp.where(lane == jnp.where(row == 0, 0, cols - 1), 1.0, 0.0).astype(jnp.bfloat16)
    for start in range(0, layers, part):
        cells = volume_ref[start:start + part].reshape(part * rows, cols)
        both = lax.dot_general(unit, cells, (((1,), (1,)), ((), ())), preferred_element_type=F32)
        first_ref[:, start * rows:(start + part) * rows] = both[0:1]
        last_ref[:, start * rows:(start + part) * rows] = both[1:2]


def ends(volume):
    layers, rows, cols = volume.shape
    out = jax.ShapeDtypeStruct((1, layers * rows), F32)
    first, last = pl.pallas_call(
        ends_kernel,
        out_shape=[out, out],
        compiler_params=pltpu.CompilerParams(vmem_limit_bytes=32 * 1024 * 1024),
        name="ends",
    )(volume)
    return first.reshape(-1, LANES), last.reshape(-1, LANES)


def body(volume, tf_color, tf_opacity, active):
    layers = volume.shape[0]
    bricks = layers // BZ
    across, down, depth = (lax.axis_size(name) for name in ("gx", "gy", "gz"))
    opacity = tf_opacity.reshape(1, -1)
    flags = active.reshape(bricks)
    column, last = ends(volume)
    rim = lax.ppermute(last, "gx", [(i, i + 1) for i in range(across - 1)])
    front, tail = render(flags, tf_color, opacity, volume)
    rows = deal(flags, tf_color, opacity, column, rim, front, tail)
    swapped = lax.all_to_all(rows.reshape(depth, 1, -1), "gz", 0, 0, tiled=True)
    merged = along_depth(swapped.reshape(-1, LANES), across, down, depth)
    arrived = lax.all_to_all(merged.reshape(across * down, 1, -1), ("gx", "gy"), 0, 0, tiled=True)
    return gather(arrived.reshape(-1, LANES), across, down)


def solution(mesh):
    placed = (P("gz", "gy", "gx"), P(), P(), P("gz", "gy", "gx"))
    return jax.shard_map(
        body,
        mesh=mesh,
        in_specs=placed,
        out_specs=P(None, ("gx", "gy", "gz"), None),
        check_vma=False,
    )
```

```python
import functools

import jax
import jax.numpy as jnp
from jax import lax
from jax.experimental import pallas as pl
from jax.experimental.pallas import tpu as pltpu
from jax.sharding import PartitionSpec as P

BZ = 8
LIMIT = 3.0
KNOTS = 16
LANES = 128
GROUP = 16
STEPS = 4
UNROLL = 4
CHAINED = (2, 5)
F32 = jnp.float32


def lane_ids(rows):
    return lax.broadcasted_iota(jnp.int32, (rows, LANES), 1)


def pick(table, index):
    return jnp.take_along_axis(table, index, axis=1, mode="promise_in_bounds")


def code_step(opacity, layers):
    clear = 1.0 - jnp.max(opacity, axis=1, keepdims=True)
    left = jnp.ones_like(clear)
    while layers:
        if layers % 2:
            left = left * clear
        clear = clear * clear
        layers //= 2
    return (1.0 - left) * (1.0 / 65500.0)


def pack(even, odd, step):
    per = 1.0 / step
    low = (even * per + 0.5).astype(jnp.int32)
    high = (odd * per + 0.5).astype(jnp.int32)
    return lax.shift_left(high, 16) | low


def unpack(word, step):
    low = (word & 0xFFFF).astype(F32) * step
    high = lax.shift_right_logical(word, 16).astype(F32) * step
    return low, high


def build_tables(color_ref, opacity_ref, pad_ref, table_ref):
    pad_ref[...] = jnp.zeros_like(pad_ref)
    pad_ref[0:3, 0:KNOTS] = color_ref[...]
    pad_ref[3:4, 0:KNOTS] = opacity_ref[...]
    upper = pad_ref[...]
    lower = pltpu.roll(upper, 1, 1)
    slope = upper - lower
    base = lower - slope * lane_ids(8).astype(F32)
    for n in range(4):
        table_ref[n] = jnp.broadcast_to(base[n:n + 1], (GROUP, LANES))
        table_ref[4 + n] = jnp.broadcast_to(slope[n:n + 1], (GROUP, LANES))


def classify(values, tables):
    scale = (KNOTS - 1) / (2.0 * LIMIT)
    place = jnp.clip(values * scale + (LIMIT * scale + 1.0), 0.0, KNOTS + 1.0)
    index = place.astype(jnp.int32)
    got = [pick(table, index) for table in tables]
    return [got[n] + got[4 + n] * place for n in range(4)]


def climb(values, knot_ref):
    scale = (KNOTS - 1) / (2.0 * LIMIT)
    place = values * scale + (LIMIT * scale + 1.0)
    base = [jnp.zeros_like(values) for n in range(4)]
    slope = [knot_ref[4 + n, 0] for n in range(4)]
    for k in range(KNOTS + 2):
        above = place >= float(k)
        for n in range(4):
            if k:
                base[n] = jnp.where(above, knot_ref[n, k], base[n])
            slope[n] = jnp.where(above, knot_ref[4 + n, k], slope[n] if k else 0.0)
    return [base[n] + slope[n] * place for n in range(4)]


def render_kernel(flag_ref, color_ref, opacity_ref, volume_ref, front_ref, tail_ref,
                  pad_ref, table_ref, run_ref, done_ref, seen_ref, knot_ref):
    step = pl.program_id(0)
    rows_all = front_ref.shape[1]
    groups = rows_all // GROUP
    bricks = volume_ref.shape[0] // BZ

    @pl.when(step == 0)
    def _():
        build_tables(color_ref, opacity_ref, pad_ref, table_ref)
        for n in range(8):
            for k in range(KNOTS + 2):
                knot_ref[n, k] = pick(table_ref[n, 0:8], jnp.full((8, LANES), k, jnp.int32))
        for ref in (run_ref, done_ref):
            ref[0:3] = jnp.zeros((3, rows_all, LANES), F32)
            ref[3] = jnp.ones((rows_all, LANES), F32)

    lane = lane_ids(GROUP)
    layers = volume_ref.shape[0]

    def look(layer, carry):
        tables = [table_ref[n, 0:8] for n in range(8)]
        for start in range(0, rows_all, GROUP):
            pair = volume_ref[layer, start:start + GROUP, :].astype(F32)
            for q in range(0, GROUP, 8):
                at = start + q
                if at // 8 in CHAINED:
                    found = climb(pair[q:q + 8], knot_ref)
                else:
                    found = classify(pair[q:q + 8], tables)
                for n in range(4):
                    seen_ref[n, layer, at:at + 8, :] = found[n]
        return carry

    lax.fori_loop(0, layers, look, 0, unroll=UNROLL)

    def one(local, carry):
        brick = step * bricks + local
        for group in range(groups):
            rows = slice(group * GROUP, (group + 1) * GROUP)
            for k in range(BZ):
                f = k / BZ
                *shades, alpha = [seen_ref[n, local * BZ + k, rows, :] for n in range(4)]
                if k == 0:
                    here = [alpha * shade for shade in shades]
                    clear = 1.0 - alpha
                    continue
                moved = alpha * f
                kept = alpha - moved
                weight = clear * kept
                beside = pltpu.roll(clear, LANES - 1, 1) * moved
                here = [h + weight * shade for h, shade in zip(here, shades)]
                if k == 1:
                    right = [beside * shade for shade in shades]
                else:
                    right = [r + beside * shade for r, shade in zip(right, shades)]
                clear = clear - clear * (kept + pltpu.roll(moved, 1, 1))
            flag = flag_ref[brick].astype(F32)
            shown = jnp.where(lane == 0, 0.0, flag)
            passed = jnp.where(lane == LANES - 1, 0.0, flag)
            image = [pltpu.roll(h * shown, brick, 1) + pltpu.roll(r * passed, brick + 1, 1)
                     for h, r in zip(here, right)]
            image.append(pltpu.roll((1.0 - clear) * shown, brick, 1))
            leaving = lane == brick - 1
            through = run_ref[3, rows, :]
            done_ref[3, rows, :] = jnp.where(leaving, through, done_ref[3, rows, :])
            through = jnp.where(leaving, 1.0, through)
            for n in range(3):
                sum_n = run_ref[n, rows, :]
                done_ref[n, rows, :] = jnp.where(leaving, sum_n, done_ref[n, rows, :])
                run_ref[n, rows, :] = jnp.where(leaving, 0.0, sum_n) + through * image[n]
            run_ref[3, rows, :] = through - through * image[3]
        return carry

    lax.fori_loop(0, bricks, one, 0)

    @pl.when(step == pl.num_programs(0) - 1)
    def _():
        wide = lane_ids(rows_all)
        total = pl.num_programs(0) * bricks
        for n in range(4):
            last = run_ref[n] if n < 3 else 1.0 - run_ref[n]
            first = done_ref[n] if n < 3 else 1.0 - done_ref[n]
            front_ref[n] = jnp.where(wide < total - 1, first, last)
            tail_ref[n] = jnp.where(wide < total - 1, last, 0.0)


def render(active, tf_color, tf_opacity, volume):
    layers, rows, cols = volume.shape
    out = jax.ShapeDtypeStruct((4, rows, LANES), F32)
    whole = pl.BlockSpec((4, rows, LANES), lambda i: (0, 0, 0))
    return pl.pallas_call(
        render_kernel,
        grid=(STEPS,),
        in_specs=[
            pl.BlockSpec(memory_space=pltpu.SMEM),
            pl.BlockSpec(tf_color.shape, lambda i: (0, 0)),
            pl.BlockSpec(tf_opacity.shape, lambda i: (0, 0)),
            pl.BlockSpec((layers // STEPS, rows, cols), lambda i: (i, 0, 0)),
        ],
        out_specs=[whole, whole],
        out_shape=[out, out],
        scratch_shapes=[
            pltpu.VMEM((8, LANES), F32),
            pltpu.VMEM((8, GROUP, LANES), F32),
            pltpu.VMEM((4, rows, LANES), F32),
            pltpu.VMEM((4, rows, LANES), F32),
            pltpu.VMEM((4, layers // STEPS, rows, LANES), F32),
            pltpu.VMEM((8, KNOTS + 2, 8, LANES), F32),
        ],
        cost_estimate=pl.CostEstimate(flops=40_000_000, bytes_accessed=2_400_000, transcendentals=0),
        compiler_params=pltpu.CompilerParams(vmem_limit_bytes=32 * 1024 * 1024),
        name="render",
    )(active, tf_color, tf_opacity, volume)


def rim_image(column_ref, rim_ref, flag_ref, tables, rows):
    pairs = BZ * rows // LANES
    bricks = column_ref.shape[0] // pairs
    lane = lane_ids(bricks)
    second = lane >= rows
    deep = lax.broadcasted_iota(jnp.int32, (bricks, LANES), 0)
    flags = jnp.zeros((bricks, LANES), F32)
    for b in range(bricks):
        flags = jnp.where(deep == b, flag_ref[b].astype(F32), flags)
    image = [jnp.zeros((bricks, LANES), F32) for c in range(4)]
    clear = jnp.ones((bricks, LANES), F32)
    for pair in range(pairs):
        f = jnp.where(second, (2 * pair + 1) / BZ, 2 * pair / BZ)
        *own, alpha = classify(column_ref[pl.ds(pair, bricks, stride=pairs), :], tables)
        *left, beside = classify(rim_ref[pl.ds(pair, bricks, stride=pairs), :], tables)
        kept = (1.0 - f) * alpha
        moved = f * beside
        sample = [kept * a + moved * b for a, b in zip(own, left)] + [kept + moved]
        for part in (sample, [pltpu.roll(value, rows, 1) for value in sample]):
            image = [total + clear * value for total, value in zip(image, part)]
            clear = clear - clear * part[3]
    return [value * flags for value in image]


def deal_kernel(layers, flag_ref, color_ref, opacity_ref, column_ref, rim_ref, front_ref, tail_ref, out_ref,
                pad_ref, table_ref):
    build_tables(color_ref, opacity_ref, pad_ref, table_ref)
    tables = [table_ref[n] for n in range(8)]
    step = code_step(opacity_ref[...], layers)
    rows = front_ref.shape[1]
    half = rows // 2
    lane = lane_ids(GROUP)
    to_alpha = lane % half + 3 * half
    rim = rim_image(column_ref, rim_ref, flag_ref, tables, rows)
    pieces = LANES // GROUP + 1
    near, far, image = [], [], []
    for parity in range(2):
        spread = [pick(value, lane % half * 2 + parity) for value in rim]
        image.append(jnp.where(lane < half, spread[0], jnp.where(
            lane < 2 * half, spread[1], jnp.where(lane < 3 * half, spread[2], spread[3]))))
        near.append(jnp.concatenate([front_ref[n, pl.ds(parity, half, stride=2), :] for n in range(4)], axis=0).T)
        far.append(jnp.concatenate([tail_ref[n, pl.ds(parity, half, stride=2), :] for n in range(4)], axis=0).T)
    for m in range(pieces):
        pair = [n[m * GROUP:(m + 1) * GROUP] if m < pieces - 1 else f[:GROUP] for n, f in zip(near, far)]
        if m == 0:
            pair = [piece + (1.0 - pick(piece, to_alpha)) * late for piece, late in zip(pair, image)]
        out_ref[pl.ds(m, GROUP, stride=pieces), :] = pack(*pair, step)


def deal(layers, flags, tf_color, tf_opacity, column, rim, front, tail):
    vmem = pl.BlockSpec(memory_space=pltpu.VMEM)
    return pl.pallas_call(
        functools.partial(deal_kernel, layers),
        in_specs=[pl.BlockSpec(memory_space=pltpu.SMEM)] + [vmem] * 6,
        out_specs=vmem,
        out_shape=jax.ShapeDtypeStruct((LANES + GROUP, LANES), jnp.int32),
        scratch_shapes=[
            pltpu.VMEM((8, LANES), F32),
            pltpu.VMEM((8, GROUP, LANES), F32),
        ],
        compiler_params=pltpu.CompilerParams(vmem_limit_bytes=32 * 1024 * 1024),
        name="deal",
    )(flags, tf_color, tf_opacity, column, rim, front, tail)


def along_depth_kernel(across, down, depth, layers, opacity_ref, arrived_ref, out_ref, total_ref, clear_ref):
    taken = arrived_ref.shape[0] // depth
    step = code_step(opacity_ref[...], layers)
    total_ref[...] = jnp.zeros_like(total_ref)
    clear_ref[...] = jnp.ones_like(clear_ref)
    quarter = LANES // 4
    lane = lane_ids(taken)
    to_alpha = lane % quarter + 3 * quarter
    for z in range(depth):
        place = slice(z, z + taken)
        for parity, piece in enumerate(unpack(arrived_ref[z * taken:(z + 1) * taken, :], step)):
            alpha = pick(piece, to_alpha)
            clear = clear_ref[parity, place, :]
            total_ref[parity, place, :] = total_ref[parity, place, :] + clear * piece
            clear_ref[parity, place, :] = clear - clear * alpha
    blocks = [[total_ref[parity, q * down:(q + 1) * down, :] for q in range(3)] for parity in range(2)]
    empty = jnp.zeros((down, LANES), F32)
    even, odd = blocks[0] + [empty], blocks[1] + [empty]
    step = code_step(opacity_ref[...], layers * depth)
    x = lax.axis_index("gx")
    for q in range(across):
        place = lax.rem(x + q, across) * down
        out_ref[pl.ds(pl.multiple_of(place, down), down), :] = pack(even[q], odd[(q + 2) % 4], step)


def along_depth(layers, tf_opacity, arrived, across, down, depth):
    return pl.pallas_call(
        functools.partial(along_depth_kernel, across, down, depth, layers),
        out_shape=jax.ShapeDtypeStruct((across * down, LANES), jnp.int32),
        scratch_shapes=[pltpu.VMEM((2, 3 * down, LANES), F32), pltpu.VMEM((2, 3 * down, LANES), F32)],
        compiler_params=pltpu.CompilerParams(vmem_limit_bytes=32 * 1024 * 1024),
        name="along_depth",
    )(tf_opacity, arrived)


def gather_kernel(across, down, layers, opacity_ref, arrived_ref, out_ref):
    step = code_step(opacity_ref[...], layers)
    me = lax.axis_index("gx")
    half = LANES // 4
    lane = lane_ids(down)
    to_alpha = lane % half + 3 * half
    total = [jnp.zeros((down, LANES), F32) for k in range(3)]
    clear = [jnp.ones((down, LANES), F32) for k in range(3)]
    for x in reversed(range(across)):
        slots = (jnp.where(me < x, 1, 0), jnp.where(me >= x + 2, 1, 2))
        for parity, piece in enumerate(unpack(arrived_ref[x * down:(x + 1) * down, :], step)):
            alpha = pick(piece, to_alpha)
            for k in range(2) if parity == 0 else range(1, 3):
                mine = jnp.where(slots[parity] == k, 1.0, 0.0)
                total[k] = total[k] + clear[k] * (piece * mine)
                clear[k] = clear[k] - clear[k] * (alpha * mine)
    width = 3 * half
    third = lane % 3
    for c in range(4):
        source = jnp.minimum(lane // 3, half - 1) + c * half
        spread = [pick(value, source) for value in total]
        row = jnp.where(third == 0, spread[0], jnp.where(third == 1, spread[1], spread[2]))
        for y in range(down):
            out_ref[c, 0:1, y * width:(y + 1) * width] = row[y:y + 1, 0:width]


def gather(layers, tf_opacity, arrived, across, down):
    pixels = down * 3 * LANES // 4
    return pl.pallas_call(
        functools.partial(gather_kernel, across, down, layers),
        out_shape=jax.ShapeDtypeStruct((4, 1, pixels), F32),
        compiler_params=pltpu.CompilerParams(vmem_limit_bytes=32 * 1024 * 1024),
        name="gather",
    )(tf_opacity, arrived)


def ends_kernel(volume_ref, first_ref, last_ref):
    layers, rows, cols = volume_ref.shape
    part = 16
    row = lax.broadcasted_iota(jnp.int32, (16, cols), 0)
    lane = lax.broadcasted_iota(jnp.int32, (16, cols), 1)
    unit = jnp.where(lane == jnp.where(row == 0, 0, cols - 1), 1.0, 0.0).astype(jnp.bfloat16)
    for start in range(0, layers, part):
        cells = volume_ref[start:start + part].reshape(part * rows, cols)
        both = lax.dot_general(unit, cells, (((1,), (1,)), ((), ())), preferred_element_type=F32)
        first_ref[:, start * rows:(start + part) * rows] = both[0:1]
        last_ref[:, start * rows:(start + part) * rows] = both[1:2]


def ends(volume):
    layers, rows, cols = volume.shape
    out = jax.ShapeDtypeStruct((1, layers * rows), F32)
    first, last = pl.pallas_call(
        ends_kernel,
        out_shape=[out, out],
        compiler_params=pltpu.CompilerParams(vmem_limit_bytes=32 * 1024 * 1024),
        name="ends",
    )(volume)
    return first.reshape(-1, LANES), last.reshape(-1, LANES)


def body(volume, tf_color, tf_opacity, active):
    layers = volume.shape[0]
    bricks = layers // BZ
    across, down, depth = (lax.axis_size(name) for name in ("gx", "gy", "gz"))
    opacity = tf_opacity.reshape(1, -1)
    flags = active.reshape(bricks)
    column, last = ends(volume)
    rim = lax.ppermute(last, "gx", [(i, i + 1) for i in range(across - 1)])
    front, tail = render(flags, tf_color, opacity, volume)
    rows = deal(layers, flags, tf_color, opacity, column, rim, front, tail)
    swapped = lax.all_to_all(rows.reshape(depth, 1, -1), "gz", 0, 0, tiled=True)
    merged = along_depth(layers, opacity, swapped.reshape(-1, LANES), across, down, depth)
    arrived = lax.all_to_all(merged.reshape(across * down, 1, -1), ("gx", "gy"), 0, 0, tiled=True)
    return gather(layers * depth, opacity, arrived.reshape(-1, LANES), across, down)


def solution(mesh):
    placed = (P("gz", "gy", "gx"), P(), P(), P("gz", "gy", "gx"))
    return jax.shard_map(
        body,
        mesh=mesh,
        in_specs=placed,
        out_specs=P(None, ("gx", "gy", "gz"), None),
        check_vma=False,
    )
```

```python
import functools

import jax
import jax.numpy as jnp
from jax import lax
from jax.experimental import pallas as pl
from jax.experimental.pallas import tpu as pltpu
from jax.sharding import PartitionSpec as P

BZ = 8
LIMIT = 3.0
KNOTS = 16
LANES = 128
GROUP = 16
STEPS = 4
UNROLL = 4
F32 = jnp.float32


def lane_ids(rows):
    return lax.broadcasted_iota(jnp.int32, (rows, LANES), 1)


def pick(table, index):
    return jnp.take_along_axis(table, index, axis=1, mode="promise_in_bounds")


def code_step(opacity, layers):
    clear = 1.0 - jnp.max(opacity, axis=1, keepdims=True)
    left = jnp.ones_like(clear)
    while layers:
        if layers % 2:
            left = left * clear
        clear = clear * clear
        layers //= 2
    return (1.0 - left) * (1.0 / 65500.0)


def pack(even, odd, step):
    per = 1.0 / step
    low = (even * per + 0.5).astype(jnp.int32)
    high = (odd * per + 0.5).astype(jnp.int32)
    return lax.shift_left(high, 16) | low


def unpack(word, step):
    low = (word & 0xFFFF).astype(F32) * step
    high = lax.shift_right_logical(word, 16).astype(F32) * step
    return low, high


def build_tables(color_ref, opacity_ref, pad_ref, table_ref):
    pad_ref[...] = jnp.zeros_like(pad_ref)
    pad_ref[0:3, 0:KNOTS] = color_ref[...]
    pad_ref[3:4, 0:KNOTS] = opacity_ref[...]
    knots = pad_ref[...]
    lane = lane_ids(8)
    slope = jnp.where(lane < KNOTS - 1, pltpu.roll(knots, LANES - 1, 1) - knots, 0.0)
    base = knots - slope * lane.astype(F32)
    row = lax.broadcasted_iota(jnp.int32, (8, LANES), 0)
    for half in range(2):
        for n in range(4):
            for m, source in enumerate((base, slope)):
                spread = jnp.broadcast_to(source[n:n + 1], (8, LANES))
                table_ref[half, m * 4 + n] = pick(spread, row + 8 * half)


def read_tables(table_ref):
    return [[table_ref[half, n] for n in range(8)] for half in range(2)]


def classify(values, tables):
    scale = (KNOTS - 1) / (2.0 * LIMIT)
    parts = []
    for start in range(0, values.shape[0], 8):
        value = values[start:start + 8]
        along = value * scale + LIMIT * scale
        place = jnp.clip(along, 0.0, KNOTS - 1.0)
        fade = jnp.maximum(1.0 - jnp.abs(along - place), 0.0)
        index = place.astype(jnp.int32)
        upper = index >= 8
        index = index & 7
        found = [jnp.where(upper, take(high, index), take(low, index)) for low, high in zip(*tables)]
        parts.append([found[n] + found[4 + n] * place for n in range(4)] + [fade])
    return [jnp.concatenate(part, axis=0) for part in zip(*parts)]


def take(table, index):
    return jnp.take_along_axis(table, index, axis=0, mode="promise_in_bounds")


def render_kernel(flag_ref, color_ref, opacity_ref, volume_ref, front_ref, tail_ref,
                  pad_ref, table_ref, run_ref, done_ref):
    step = pl.program_id(0)
    rows_all = front_ref.shape[1]
    groups = rows_all // GROUP
    bricks = volume_ref.shape[0] // BZ

    @pl.when(step == 0)
    def _():
        build_tables(color_ref, opacity_ref, pad_ref, table_ref)
        for ref in (run_ref, done_ref):
            ref[0:3] = jnp.zeros((3, rows_all, LANES), F32)
            ref[3] = jnp.ones((rows_all, LANES), F32)

    lane = lane_ids(GROUP)
    def one(item, carry):
        tables = read_tables(table_ref)
        local = item // groups
        brick = step * bricks + local
        rows = pl.ds(pl.multiple_of(item % groups * GROUP, GROUP), GROUP)
        for k in range(BZ):
            f = k / BZ
            *shades, alpha, fade = classify(volume_ref[local * BZ + k, rows, :].astype(F32), tables)
            alpha = alpha * fade
            if k == 0:
                weight = alpha * fade
                here = [weight * shade for shade in shades]
                clear = 1.0 - alpha
                continue
            moved = alpha * f
            kept = alpha - moved
            weight = clear * kept * fade
            beside = pltpu.roll(clear, LANES - 1, 1) * moved * fade
            here = [h + weight * shade for h, shade in zip(here, shades)]
            if k == 1:
                right = [beside * shade for shade in shades]
            else:
                right = [r + beside * shade for r, shade in zip(right, shades)]
            clear = clear - clear * (kept + pltpu.roll(moved, 1, 1))
        flag = flag_ref[brick].astype(F32)
        shown = jnp.where(lane == 0, 0.0, flag)
        passed = jnp.where(lane == LANES - 1, 0.0, flag)
        image = [pltpu.roll(h * shown, brick, 1) + pltpu.roll(r * passed, brick + 1, 1)
                 for h, r in zip(here, right)]
        image.append(pltpu.roll((1.0 - clear) * shown, brick, 1))
        leaving = lane == brick - 1
        through = run_ref[3, rows, :]
        done_ref[3, rows, :] = jnp.where(leaving, through, done_ref[3, rows, :])
        through = jnp.where(leaving, 1.0, through)
        for n in range(3):
            sum_n = run_ref[n, rows, :]
            done_ref[n, rows, :] = jnp.where(leaving, sum_n, done_ref[n, rows, :])
            run_ref[n, rows, :] = jnp.where(leaving, 0.0, sum_n) + through * image[n]
        run_ref[3, rows, :] = through - through * image[3]
        return carry

    lax.fori_loop(0, bricks * groups, one, 0, unroll=UNROLL)

    @pl.when(step == pl.num_programs(0) - 1)
    def _():
        wide = lane_ids(rows_all)
        total = pl.num_programs(0) * bricks
        for n in range(4):
            last = run_ref[n] if n < 3 else 1.0 - run_ref[n]
            first = done_ref[n] if n < 3 else 1.0 - done_ref[n]
            front_ref[n] = jnp.where(wide < total - 1, first, last)
            tail_ref[n] = jnp.where(wide < total - 1, last, 0.0)


def render(active, tf_color, tf_opacity, volume):
    layers, rows, cols = volume.shape
    out = jax.ShapeDtypeStruct((4, rows, LANES), F32)
    whole = pl.BlockSpec((4, rows, LANES), lambda i: (0, 0, 0))
    return pl.pallas_call(
        render_kernel,
        grid=(STEPS,),
        in_specs=[
            pl.BlockSpec(memory_space=pltpu.SMEM),
            pl.BlockSpec(tf_color.shape, lambda i: (0, 0)),
            pl.BlockSpec(tf_opacity.shape, lambda i: (0, 0)),
            pl.BlockSpec((layers // STEPS, rows, cols), lambda i: (i, 0, 0)),
        ],
        out_specs=[whole, whole],
        out_shape=[out, out],
        scratch_shapes=[
            pltpu.VMEM((8, LANES), F32),
            pltpu.VMEM((2, 8, 8, LANES), F32),
            pltpu.VMEM((4, rows, LANES), F32),
            pltpu.VMEM((4, rows, LANES), F32),
        ],
        cost_estimate=pl.CostEstimate(flops=40_000_000, bytes_accessed=2_400_000, transcendentals=0),
        compiler_params=pltpu.CompilerParams(vmem_limit_bytes=32 * 1024 * 1024),
        name="render",
    )(active, tf_color, tf_opacity, volume)


def rim_image(column_ref, rim_ref, flag_ref, tables, rows):
    pairs = BZ * rows // LANES
    bricks = column_ref.shape[0] // pairs
    lane = lane_ids(bricks)
    second = lane >= rows
    deep = lax.broadcasted_iota(jnp.int32, (bricks, LANES), 0)
    flags = jnp.zeros((bricks, LANES), F32)
    for b in range(bricks):
        flags = jnp.where(deep == b, flag_ref[b].astype(F32), flags)
    image = [jnp.zeros((bricks, LANES), F32) for c in range(4)]
    clear = jnp.ones((bricks, LANES), F32)
    for pair in range(pairs):
        f = jnp.where(second, (2 * pair + 1) / BZ, 2 * pair / BZ)
        *own, alpha, fade = classify(column_ref[pl.ds(pair, bricks, stride=pairs), :], tables)
        *left, beside, side_fade = classify(rim_ref[pl.ds(pair, bricks, stride=pairs), :], tables)
        kept = (1.0 - f) * (alpha * fade)
        moved = f * (beside * side_fade)
        sample = [kept * fade * a + moved * side_fade * b for a, b in zip(own, left)] + [kept + moved]
        for part in (sample, [pltpu.roll(value, rows, 1) for value in sample]):
            image = [total + clear * value for total, value in zip(image, part)]
            clear = clear - clear * part[3]
    return [value * flags for value in image]


def deal_kernel(layers, flag_ref, color_ref, opacity_ref, column_ref, rim_ref, front_ref, tail_ref, out_ref,
                pad_ref, table_ref):
    build_tables(color_ref, opacity_ref, pad_ref, table_ref)
    tables = read_tables(table_ref)
    step = code_step(opacity_ref[...], layers)
    rows = front_ref.shape[1]
    half = rows // 2
    lane = lane_ids(GROUP)
    to_alpha = lane % half + 3 * half
    rim = rim_image(column_ref, rim_ref, flag_ref, tables, rows)
    pieces = LANES // GROUP + 1
    near, far, image = [], [], []
    for parity in range(2):
        spread = [pick(value, lane % half * 2 + parity) for value in rim]
        image.append(jnp.where(lane < half, spread[0], jnp.where(
            lane < 2 * half, spread[1], jnp.where(lane < 3 * half, spread[2], spread[3]))))
        near.append(jnp.concatenate([front_ref[n, pl.ds(parity, half, stride=2), :] for n in range(4)], axis=0).T)
        far.append(jnp.concatenate([tail_ref[n, pl.ds(parity, half, stride=2), :] for n in range(4)], axis=0).T)
    for m in range(pieces):
        pair = [n[m * GROUP:(m + 1) * GROUP] if m < pieces - 1 else f[:GROUP] for n, f in zip(near, far)]
        if m == 0:
            pair = [piece + (1.0 - pick(piece, to_alpha)) * late for piece, late in zip(pair, image)]
        out_ref[pl.ds(m, GROUP, stride=pieces), :] = pack(*pair, step)


def deal(layers, flags, tf_color, tf_opacity, column, rim, front, tail):
    vmem = pl.BlockSpec(memory_space=pltpu.VMEM)
    return pl.pallas_call(
        functools.partial(deal_kernel, layers),
        in_specs=[pl.BlockSpec(memory_space=pltpu.SMEM)] + [vmem] * 6,
        out_specs=vmem,
        out_shape=jax.ShapeDtypeStruct((LANES + GROUP, LANES), jnp.int32),
        scratch_shapes=[
            pltpu.VMEM((8, LANES), F32),
            pltpu.VMEM((2, 8, 8, LANES), F32),
        ],
        compiler_params=pltpu.CompilerParams(vmem_limit_bytes=32 * 1024 * 1024),
        name="deal",
    )(flags, tf_color, tf_opacity, column, rim, front, tail)


def along_depth_kernel(across, down, depth, layers, opacity_ref, arrived_ref, out_ref, total_ref, clear_ref):
    taken = arrived_ref.shape[0] // depth
    step = code_step(opacity_ref[...], layers)
    total_ref[...] = jnp.zeros_like(total_ref)
    clear_ref[...] = jnp.ones_like(clear_ref)
    quarter = LANES // 4
    lane = lane_ids(taken)
    to_alpha = lane % quarter + 3 * quarter
    for z in range(depth):
        place = slice(z, z + taken)
        for parity, piece in enumerate(unpack(arrived_ref[z * taken:(z + 1) * taken, :], step)):
            alpha = pick(piece, to_alpha)
            clear = clear_ref[parity, place, :]
            total_ref[parity, place, :] = total_ref[parity, place, :] + clear * piece
            clear_ref[parity, place, :] = clear - clear * alpha
    blocks = [[total_ref[parity, q * down:(q + 1) * down, :] for q in range(3)] for parity in range(2)]
    empty = jnp.zeros((down, LANES), F32)
    even, odd = blocks[0] + [empty], blocks[1] + [empty]
    step = code_step(opacity_ref[...], layers * depth)
    x = lax.axis_index("gx")
    for q in range(across):
        place = lax.rem(x + q, across) * down
        out_ref[pl.ds(pl.multiple_of(place, down), down), :] = pack(even[q], odd[(q + 2) % 4], step)


def along_depth(layers, tf_opacity, arrived, across, down, depth):
    return pl.pallas_call(
        functools.partial(along_depth_kernel, across, down, depth, layers),
        out_shape=jax.ShapeDtypeStruct((across * down, LANES), jnp.int32),
        scratch_shapes=[pltpu.VMEM((2, 3 * down, LANES), F32), pltpu.VMEM((2, 3 * down, LANES), F32)],
        compiler_params=pltpu.CompilerParams(vmem_limit_bytes=32 * 1024 * 1024),
        name="along_depth",
    )(tf_opacity, arrived)


def gather_kernel(across, down, layers, opacity_ref, arrived_ref, out_ref):
    step = code_step(opacity_ref[...], layers)
    me = lax.axis_index("gx")
    half = LANES // 4
    lane = lane_ids(down)
    to_alpha = lane % half + 3 * half
    total = [jnp.zeros((down, LANES), F32) for k in range(3)]
    clear = [jnp.ones((down, LANES), F32) for k in range(3)]
    for x in reversed(range(across)):
        slots = (jnp.where(me < x, 1, 0), jnp.where(me >= x + 2, 1, 2))
        for parity, piece in enumerate(unpack(arrived_ref[x * down:(x + 1) * down, :], step)):
            alpha = pick(piece, to_alpha)
            for k in range(2) if parity == 0 else range(1, 3):
                mine = jnp.where(slots[parity] == k, 1.0, 0.0)
                total[k] = total[k] + clear[k] * (piece * mine)
                clear[k] = clear[k] - clear[k] * (alpha * mine)
    width = 3 * half
    third = lane % 3
    for c in range(4):
        source = jnp.minimum(lane // 3, half - 1) + c * half
        spread = [pick(value, source) for value in total]
        row = jnp.where(third == 0, spread[0], jnp.where(third == 1, spread[1], spread[2]))
        for y in range(down):
            out_ref[c, 0:1, y * width:(y + 1) * width] = row[y:y + 1, 0:width]


def gather(layers, tf_opacity, arrived, across, down):
    pixels = down * 3 * LANES // 4
    return pl.pallas_call(
        functools.partial(gather_kernel, across, down, layers),
        out_shape=jax.ShapeDtypeStruct((4, 1, pixels), F32),
        compiler_params=pltpu.CompilerParams(vmem_limit_bytes=32 * 1024 * 1024),
        name="gather",
    )(tf_opacity, arrived)


def ends_kernel(volume_ref, first_ref, last_ref):
    layers, rows, cols = volume_ref.shape
    part = 16
    row = lax.broadcasted_iota(jnp.int32, (16, cols), 0)
    lane = lax.broadcasted_iota(jnp.int32, (16, cols), 1)
    unit = jnp.where(lane == jnp.where(row == 0, 0, cols - 1), 1.0, 0.0).astype(jnp.bfloat16)
    for start in range(0, layers, part):
        cells = volume_ref[start:start + part].reshape(part * rows, cols)
        both = lax.dot_general(unit, cells, (((1,), (1,)), ((), ())), preferred_element_type=F32)
        first_ref[:, start * rows:(start + part) * rows] = both[0:1]
        last_ref[:, start * rows:(start + part) * rows] = both[1:2]


def ends(volume):
    layers, rows, cols = volume.shape
    out = jax.ShapeDtypeStruct((1, layers * rows), F32)
    first, last = pl.pallas_call(
        ends_kernel,
        out_shape=[out, out],
        compiler_params=pltpu.CompilerParams(vmem_limit_bytes=32 * 1024 * 1024),
        name="ends",
    )(volume)
    return first.reshape(-1, LANES), last.reshape(-1, LANES)


def body(volume, tf_color, tf_opacity, active):
    layers = volume.shape[0]
    bricks = layers // BZ
    across, down, depth = (lax.axis_size(name) for name in ("gx", "gy", "gz"))
    opacity = tf_opacity.reshape(1, -1)
    flags = active.reshape(bricks)
    column, last = ends(volume)
    rim = lax.ppermute(last, "gx", [(i, i + 1) for i in range(across - 1)])
    front, tail = render(flags, tf_color, opacity, volume)
    rows = deal(layers, flags, tf_color, opacity, column, rim, front, tail)
    swapped = lax.all_to_all(rows.reshape(depth, 1, -1), "gz", 0, 0, tiled=True)
    merged = along_depth(layers, opacity, swapped.reshape(-1, LANES), across, down, depth)
    arrived = lax.all_to_all(merged.reshape(across * down, 1, -1), ("gx", "gy"), 0, 0, tiled=True)
    return gather(layers * depth, opacity, arrived.reshape(-1, LANES), across, down)


def solution(mesh):
    placed = (P("gz", "gy", "gx"), P(), P(), P("gz", "gy", "gx"))
    return jax.shard_map(
        body,
        mesh=mesh,
        in_specs=placed,
        out_specs=P(None, ("gx", "gy", "gz"), None),
        check_vma=False,
    )
```

```python
import functools

import jax
import jax.numpy as jnp
from jax import lax
from jax.experimental import pallas as pl
from jax.experimental.pallas import tpu as pltpu
from jax.sharding import PartitionSpec as P

BZ = 8
LIMIT = 3.0
KNOTS = 16
LANES = 128
GROUP = 16
F32 = jnp.float32


def lane_ids(rows):
    return lax.broadcasted_iota(jnp.int32, (rows, LANES), 1)


def pick(table, index):
    return jnp.take_along_axis(table, index, axis=1, mode="promise_in_bounds")


def code_step(opacity, layers):
    clear = 1.0 - jnp.max(opacity, axis=1, keepdims=True)
    left = jnp.ones_like(clear)
    while layers:
        if layers % 2:
            left = left * clear
        clear = clear * clear
        layers //= 2
    return (1.0 - left) * (1.0 / 65500.0)


def pack(even, odd, step):
    per = 1.0 / step
    low = (even * per + 0.5).astype(jnp.int32)
    high = (odd * per + 0.5).astype(jnp.int32)
    return lax.shift_left(high, 16) | low


def unpack(word, step):
    low = (word & 0xFFFF).astype(F32) * step
    high = lax.shift_right_logical(word, 16).astype(F32) * step
    return low, high


def build_tables(color_ref, opacity_ref, pad_ref, table_ref):
    pad_ref[...] = jnp.zeros_like(pad_ref)
    pad_ref[0:3, 0:KNOTS] = color_ref[...]
    pad_ref[3:4, 0:KNOTS] = opacity_ref[...]
    knots = pad_ref[...]
    lane = lane_ids(8)
    slope = jnp.where(lane < KNOTS - 1, pltpu.roll(knots, LANES - 1, 1) - knots, 0.0)
    base = knots - slope * lane.astype(F32)
    row = lax.broadcasted_iota(jnp.int32, (8, LANES), 0)
    for half in range(2):
        for n in range(4):
            for m, source in enumerate((base, slope)):
                spread = jnp.broadcast_to(source[n:n + 1], (8, LANES))
                table_ref[half, m * 4 + n] = pick(spread, row + 8 * half)


def read_tables(table_ref):
    return [[table_ref[half, n] for n in range(8)] for half in range(2)]


def classify(values, tables):
    scale = (KNOTS - 1) / (2.0 * LIMIT)
    parts = []
    for start in range(0, values.shape[0], 8):
        value = values[start:start + 8]
        along = value * scale + LIMIT * scale
        place = jnp.clip(along, 0.0, KNOTS - 1.0)
        fade = jnp.maximum(1.0 - jnp.abs(along - place), 0.0)
        index = place.astype(jnp.int32)
        upper = index >= 8
        index = index & 7
        found = [jnp.where(upper, take(high, index), take(low, index)) for low, high in zip(*tables)]
        parts.append([found[n] + found[4 + n] * place for n in range(4)] + [fade])
    return [jnp.concatenate(part, axis=0) for part in zip(*parts)]


def take(table, index):
    return jnp.take_along_axis(table, index, axis=0, mode="promise_in_bounds")


def render_kernel(flag_ref, color_ref, opacity_ref, volume_ref, front_ref, tail_ref,
                  pad_ref, table_ref, run_ref, done_ref):
    rows_all = front_ref.shape[1]
    groups = rows_all // GROUP
    bricks = volume_ref.shape[0] // BZ

    build_tables(color_ref, opacity_ref, pad_ref, table_ref)
    for ref in (run_ref, done_ref):
        ref[0:3] = jnp.zeros((3, rows_all, LANES), F32)
        ref[3] = jnp.ones((rows_all, LANES), F32)

    lane = lane_ids(GROUP)

    def group_of(brick, rows):
        tables = read_tables(table_ref)
        for k in range(BZ):
            f = k / BZ
            *shades, alpha, fade = classify(volume_ref[brick * BZ + k, rows, :].astype(F32), tables)
            alpha = alpha * fade
            if k == 0:
                weight = alpha * fade
                here = [weight * shade for shade in shades]
                clear = 1.0 - alpha
                continue
            moved = alpha * f
            kept = alpha - moved
            weight = clear * kept * fade
            beside = pltpu.roll(clear, LANES - 1, 1) * moved * fade
            here = [h + weight * shade for h, shade in zip(here, shades)]
            if k == 1:
                right = [beside * shade for shade in shades]
            else:
                right = [r + beside * shade for r, shade in zip(right, shades)]
            clear = clear - clear * (kept + pltpu.roll(moved, 1, 1))
        shown = jnp.where(lane == 0, 0.0, 1.0)
        passed = jnp.where(lane == LANES - 1, 0.0, 1.0)
        image = [pltpu.roll(h * shown, brick, 1) + pltpu.roll(r * passed, brick + 1, 1)
                 for h, r in zip(here, right)]
        image.append(pltpu.roll((1.0 - clear) * shown, brick, 1))
        through = run_ref[3, rows, :]
        for n in range(3):
            run_ref[n, rows, :] = run_ref[n, rows, :] + through * image[n]
        run_ref[3, rows, :] = through - through * image[3]

    def one(brick, carry):
        leaving = lane == brick - 1
        for group in range(groups):
            rows = slice(group * GROUP, (group + 1) * GROUP)
            for n in range(4):
                value = run_ref[n, rows, :]
                done_ref[n, rows, :] = jnp.where(leaving, value, done_ref[n, rows, :])
                run_ref[n, rows, :] = jnp.where(leaving, float(n == 3), value)

        @pl.when(flag_ref[brick] > 0)
        def _():
            for group in range(groups):
                group_of(brick, slice(group * GROUP, (group + 1) * GROUP))

        return carry

    lax.fori_loop(0, bricks, one, 0)

    wide = lane_ids(rows_all)
    for n in range(4):
        last = run_ref[n] if n < 3 else 1.0 - run_ref[n]
        first = done_ref[n] if n < 3 else 1.0 - done_ref[n]
        front_ref[n] = jnp.where(wide < bricks - 1, first, last)
        tail_ref[n] = jnp.where(wide < bricks - 1, last, 0.0)


def render(active, tf_color, tf_opacity, volume):
    layers, rows, cols = volume.shape
    out = jax.ShapeDtypeStruct((4, rows, LANES), F32)
    vmem = pl.BlockSpec(memory_space=pltpu.VMEM)
    return pl.pallas_call(
        render_kernel,
        in_specs=[pl.BlockSpec(memory_space=pltpu.SMEM), vmem, vmem, vmem],
        out_specs=[vmem, vmem],
        out_shape=[out, out],
        scratch_shapes=[
            pltpu.VMEM((8, LANES), F32),
            pltpu.VMEM((2, 8, 8, LANES), F32),
            pltpu.VMEM((4, rows, LANES), F32),
            pltpu.VMEM((4, rows, LANES), F32),
        ],
        cost_estimate=pl.CostEstimate(flops=40_000_000, bytes_accessed=2_400_000, transcendentals=0),
        compiler_params=pltpu.CompilerParams(vmem_limit_bytes=32 * 1024 * 1024),
        name="render",
    )(active, tf_color, tf_opacity, volume)


def rim_image(column_ref, rim_ref, flag_ref, tables, rows):
    pairs = BZ * rows // LANES
    bricks = column_ref.shape[0] // pairs
    lane = lane_ids(bricks)
    second = lane >= rows
    deep = lax.broadcasted_iota(jnp.int32, (bricks, LANES), 0)
    flags = jnp.zeros((bricks, LANES), F32)
    for b in range(bricks):
        flags = jnp.where(deep == b, flag_ref[b].astype(F32), flags)
    image = [jnp.zeros((bricks, LANES), F32) for c in range(4)]
    clear = jnp.ones((bricks, LANES), F32)
    for pair in range(pairs):
        f = jnp.where(second, (2 * pair + 1) / BZ, 2 * pair / BZ)
        *own, alpha, fade = classify(column_ref[pl.ds(pair, bricks, stride=pairs), :], tables)
        *left, beside, side_fade = classify(rim_ref[pl.ds(pair, bricks, stride=pairs), :], tables)
        kept = (1.0 - f) * (alpha * fade)
        moved = f * (beside * side_fade)
        sample = [kept * fade * a + moved * side_fade * b for a, b in zip(own, left)] + [kept + moved]
        for part in (sample, [pltpu.roll(value, rows, 1) for value in sample]):
            image = [total + clear * value for total, value in zip(image, part)]
            clear = clear - clear * part[3]
    return [value * flags for value in image]


def deal_kernel(layers, flag_ref, color_ref, opacity_ref, column_ref, rim_ref, front_ref, tail_ref, out_ref,
                pad_ref, table_ref):
    build_tables(color_ref, opacity_ref, pad_ref, table_ref)
    tables = read_tables(table_ref)
    step = code_step(opacity_ref[...], layers)
    rows = front_ref.shape[1]
    half = rows // 2
    lane = lane_ids(GROUP)
    to_alpha = lane % half + 3 * half
    rim = rim_image(column_ref, rim_ref, flag_ref, tables, rows)
    pieces = LANES // GROUP + 1
    near, far, image = [], [], []
    for parity in range(2):
        spread = [pick(value, lane % half * 2 + parity) for value in rim]
        image.append(jnp.where(lane < half, spread[0], jnp.where(
            lane < 2 * half, spread[1], jnp.where(lane < 3 * half, spread[2], spread[3]))))
        near.append(jnp.concatenate([front_ref[n, pl.ds(parity, half, stride=2), :] for n in range(4)], axis=0).T)
        far.append(jnp.concatenate([tail_ref[n, pl.ds(parity, half, stride=2), :] for n in range(4)], axis=0).T)
    for m in range(pieces):
        pair = [n[m * GROUP:(m + 1) * GROUP] if m < pieces - 1 else f[:GROUP] for n, f in zip(near, far)]
        if m == 0:
            pair = [piece + (1.0 - pick(piece, to_alpha)) * late for piece, late in zip(pair, image)]
        out_ref[pl.ds(m, GROUP, stride=pieces), :] = pack(*pair, step)


def deal(layers, flags, tf_color, tf_opacity, column, rim, front, tail):
    vmem = pl.BlockSpec(memory_space=pltpu.VMEM)
    return pl.pallas_call(
        functools.partial(deal_kernel, layers),
        in_specs=[pl.BlockSpec(memory_space=pltpu.SMEM)] + [vmem] * 6,
        out_specs=vmem,
        out_shape=jax.ShapeDtypeStruct((LANES + GROUP, LANES), jnp.int32),
        scratch_shapes=[
            pltpu.VMEM((8, LANES), F32),
            pltpu.VMEM((2, 8, 8, LANES), F32),
        ],
        compiler_params=pltpu.CompilerParams(vmem_limit_bytes=32 * 1024 * 1024),
        name="deal",
    )(flags, tf_color, tf_opacity, column, rim, front, tail)


def along_depth_kernel(across, down, depth, layers, opacity_ref, arrived_ref, out_ref, total_ref, clear_ref):
    taken = arrived_ref.shape[0] // depth
    step = code_step(opacity_ref[...], layers)
    total_ref[...] = jnp.zeros_like(total_ref)
    clear_ref[...] = jnp.ones_like(clear_ref)
    quarter = LANES // 4
    lane = lane_ids(taken)
    to_alpha = lane % quarter + 3 * quarter
    for z in range(depth):
        place = slice(z, z + taken)
        for parity, piece in enumerate(unpack(arrived_ref[z * taken:(z + 1) * taken, :], step)):
            alpha = pick(piece, to_alpha)
            clear = clear_ref[parity, place, :]
            total_ref[parity, place, :] = total_ref[parity, place, :] + clear * piece
            clear_ref[parity, place, :] = clear - clear * alpha
    blocks = [[total_ref[parity, q * down:(q + 1) * down, :] for q in range(3)] for parity in range(2)]
    empty = jnp.zeros((down, LANES), F32)
    even, odd = blocks[0] + [empty], blocks[1] + [empty]
    step = code_step(opacity_ref[...], layers * depth)
    x = lax.axis_index("gx")
    for q in range(across):
        place = lax.rem(x + q, across) * down
        out_ref[pl.ds(pl.multiple_of(place, down), down), :] = pack(even[q], odd[(q + 2) % 4], step)


def along_depth(layers, tf_opacity, arrived, across, down, depth):
    return pl.pallas_call(
        functools.partial(along_depth_kernel, across, down, depth, layers),
        out_shape=jax.ShapeDtypeStruct((across * down, LANES), jnp.int32),
        scratch_shapes=[pltpu.VMEM((2, 3 * down, LANES), F32), pltpu.VMEM((2, 3 * down, LANES), F32)],
        compiler_params=pltpu.CompilerParams(vmem_limit_bytes=32 * 1024 * 1024),
        name="along_depth",
    )(tf_opacity, arrived)


def gather_kernel(across, down, layers, opacity_ref, arrived_ref, out_ref):
    step = code_step(opacity_ref[...], layers)
    me = lax.axis_index("gx")
    half = LANES // 4
    lane = lane_ids(down)
    to_alpha = lane % half + 3 * half
    total = [jnp.zeros((down, LANES), F32) for k in range(3)]
    clear = [jnp.ones((down, LANES), F32) for k in range(3)]
    for x in reversed(range(across)):
        slots = (jnp.where(me < x, 1, 0), jnp.where(me >= x + 2, 1, 2))
        for parity, piece in enumerate(unpack(arrived_ref[x * down:(x + 1) * down, :], step)):
            alpha = pick(piece, to_alpha)
            for k in range(2) if parity == 0 else range(1, 3):
                mine = jnp.where(slots[parity] == k, 1.0, 0.0)
                total[k] = total[k] + clear[k] * (piece * mine)
                clear[k] = clear[k] - clear[k] * (alpha * mine)
    width = 3 * half
    third = lane % 3
    for c in range(4):
        source = jnp.minimum(lane // 3, half - 1) + c * half
        spread = [pick(value, source) for value in total]
        row = jnp.where(third == 0, spread[0], jnp.where(third == 1, spread[1], spread[2]))
        for y in range(down):
            out_ref[c, 0:1, y * width:(y + 1) * width] = row[y:y + 1, 0:width]


def gather(layers, tf_opacity, arrived, across, down):
    pixels = down * 3 * LANES // 4
    return pl.pallas_call(
        functools.partial(gather_kernel, across, down, layers),
        out_shape=jax.ShapeDtypeStruct((4, 1, pixels), F32),
        compiler_params=pltpu.CompilerParams(vmem_limit_bytes=32 * 1024 * 1024),
        name="gather",
    )(tf_opacity, arrived)


def ends_kernel(volume_ref, first_ref, last_ref):
    layers, rows, cols = volume_ref.shape
    part = 16
    row = lax.broadcasted_iota(jnp.int32, (16, cols), 0)
    lane = lax.broadcasted_iota(jnp.int32, (16, cols), 1)
    unit = jnp.where(lane == jnp.where(row == 0, 0, cols - 1), 1.0, 0.0).astype(jnp.bfloat16)
    for start in range(0, layers, part):
        cells = volume_ref[start:start + part].reshape(part * rows, cols)
        both = lax.dot_general(unit, cells, (((1,), (1,)), ((), ())), preferred_element_type=F32)
        first_ref[:, start * rows:(start + part) * rows] = both[0:1]
        last_ref[:, start * rows:(start + part) * rows] = both[1:2]


def ends(volume):
    layers, rows, cols = volume.shape
    out = jax.ShapeDtypeStruct((1, layers * rows), F32)
    first, last = pl.pallas_call(
        ends_kernel,
        out_shape=[out, out],
        compiler_params=pltpu.CompilerParams(vmem_limit_bytes=32 * 1024 * 1024),
        name="ends",
    )(volume)
    return first.reshape(-1, LANES), last.reshape(-1, LANES)


def body(volume, tf_color, tf_opacity, active):
    layers = volume.shape[0]
    bricks = layers // BZ
    across, down, depth = (lax.axis_size(name) for name in ("gx", "gy", "gz"))
    opacity = tf_opacity.reshape(1, -1)
    flags = active.reshape(bricks)
    column, last = ends(volume)
    rim = lax.ppermute(last, "gx", [(i, i + 1) for i in range(across - 1)])
    front, tail = render(flags, tf_color, opacity, volume)
    rows = deal(layers, flags, tf_color, opacity, column, rim, front, tail)
    swapped = lax.all_to_all(rows.reshape(depth, 1, -1), "gz", 0, 0, tiled=True)
    merged = along_depth(layers, opacity, swapped.reshape(-1, LANES), across, down, depth)
    arrived = lax.all_to_all(merged.reshape(across * down, 1, -1), ("gx", "gy"), 0, 0, tiled=True)
    return gather(layers * depth, opacity, arrived.reshape(-1, LANES), across, down)


def solution(mesh):
    placed = (P("gz", "gy", "gx"), P(), P(), P("gz", "gy", "gx"))
    return jax.shard_map(
        body,
        mesh=mesh,
        in_specs=placed,
        out_specs=P(None, ("gx", "gy", "gz"), None),
        check_vma=False,
    )
```

```python
import functools

import jax
import jax.numpy as jnp
from jax import lax
from jax.experimental import pallas as pl
from jax.experimental.pallas import tpu as pltpu
from jax.sharding import PartitionSpec as P

BZ = 8
LIMIT = 3.0
KNOTS = 16
LANES = 128
GROUP = 16
F32 = jnp.float32


def lane_ids(rows):
    return lax.broadcasted_iota(jnp.int32, (rows, LANES), 1)


def pick(table, index):
    return jnp.take_along_axis(table, index, axis=1, mode="promise_in_bounds")


def code_step(opacity, layers):
    clear = 1.0 - jnp.max(opacity, axis=1, keepdims=True)
    left = jnp.ones_like(clear)
    while layers:
        if layers % 2:
            left = left * clear
        clear = clear * clear
        layers //= 2
    return (1.0 - left) * (1.0 / 65500.0)


def pack(even, odd, step):
    per = 1.0 / step
    low = (even * per + 0.5).astype(jnp.int32)
    high = (odd * per + 0.5).astype(jnp.int32)
    return lax.shift_left(high, 16) | low


def unpack(word, step):
    low = (word & 0xFFFF).astype(F32) * step
    high = lax.shift_right_logical(word, 16).astype(F32) * step
    return low, high


def build_tables(color_ref, opacity_ref, pad_ref, table_ref):
    pad_ref[...] = jnp.zeros_like(pad_ref)
    pad_ref[0:3, 0:KNOTS] = color_ref[...]
    pad_ref[3:4, 0:KNOTS] = opacity_ref[...]
    knots = pad_ref[...]
    lane = lane_ids(8)
    slope = jnp.where(lane < KNOTS - 1, pltpu.roll(knots, LANES - 1, 1) - knots, 0.0)
    base = knots - slope * lane.astype(F32)
    row = lax.broadcasted_iota(jnp.int32, (8, LANES), 0)
    for half in range(2):
        for n in range(4):
            for m, source in enumerate((base, slope)):
                spread = jnp.broadcast_to(source[n:n + 1], (8, LANES))
                table_ref[half, m * 4 + n] = pick(spread, row + 8 * half)


def read_tables(table_ref):
    return [[table_ref[half, n] for n in range(8)] for half in range(2)]


def classify(values, tables):
    scale = (KNOTS - 1) / (2.0 * LIMIT)
    parts = []
    for start in range(0, values.shape[0], 8):
        value = values[start:start + 8]
        along = value * scale + LIMIT * scale
        place = jnp.clip(along, 0.0, KNOTS - 1.0)
        fade = jnp.maximum(1.0 - jnp.abs(along - place), 0.0)
        index = place.astype(jnp.int32)
        upper = index >= 8
        index = index & 7
        found = [jnp.where(upper, take(high, index), take(low, index)) for low, high in zip(*tables)]
        parts.append([found[n] + found[4 + n] * place for n in range(4)] + [fade])
    return [jnp.concatenate(part, axis=0) for part in zip(*parts)]


def take(table, index):
    return jnp.take_along_axis(table, index, axis=0, mode="promise_in_bounds")


def render_kernel(flag_ref, color_ref, opacity_ref, volume_ref, run_ref, done_ref, table_ref, pad_ref):
    rows_all = run_ref.shape[1]
    groups = rows_all // GROUP
    bricks = volume_ref.shape[0] // BZ

    build_tables(color_ref, opacity_ref, pad_ref, table_ref)
    for ref in (run_ref, done_ref):
        ref[0:3] = jnp.zeros((3, rows_all, LANES), F32)
        ref[3] = jnp.ones((rows_all, LANES), F32)

    lane = lane_ids(GROUP)

    def group_of(brick, rows):
        tables = read_tables(table_ref)
        for k in range(BZ):
            f = k / BZ
            *shades, alpha, fade = classify(volume_ref[brick * BZ + k, rows, :].astype(F32), tables)
            alpha = alpha * fade
            if k == 0:
                weight = alpha * fade
                here = [weight * shade for shade in shades]
                clear = 1.0 - alpha
                continue
            moved = alpha * f
            kept = alpha - moved
            weight = clear * kept * fade
            beside = pltpu.roll(clear, LANES - 1, 1) * moved * fade
            here = [h + weight * shade for h, shade in zip(here, shades)]
            if k == 1:
                right = [beside * shade for shade in shades]
            else:
                right = [r + beside * shade for r, shade in zip(right, shades)]
            clear = clear - clear * (kept + pltpu.roll(moved, 1, 1))
        shown = jnp.where(lane == 0, 0.0, 1.0)
        passed = jnp.where(lane == LANES - 1, 0.0, 1.0)
        image = [pltpu.roll(h * shown, brick, 1) + pltpu.roll(r * passed, brick + 1, 1)
                 for h, r in zip(here, right)]
        image.append(pltpu.roll((1.0 - clear) * shown, brick, 1))
        through = run_ref[3, rows, :]
        for n in range(3):
            run_ref[n, rows, :] = run_ref[n, rows, :] + through * image[n]
        run_ref[3, rows, :] = through - through * image[3]

    def leave(first, last):
        leaving = (lane >= first) & (lane < last)
        for group in range(groups):
            rows = slice(group * GROUP, (group + 1) * GROUP)
            for n in range(4):
                value = run_ref[n, rows, :]
                done_ref[n, rows, :] = jnp.where(leaving, value, done_ref[n, rows, :])
                run_ref[n, rows, :] = jnp.where(leaving, float(n == 3), value)

    def one(brick, left):
        active = flag_ref[brick] > 0

        @pl.when(active)
        def _():
            leave(left, brick)
            for group in range(groups):
                group_of(brick, slice(group * GROUP, (group + 1) * GROUP))

        return jnp.where(active, brick, left)

    leave(lax.fori_loop(0, bricks, one, 0), bricks - 1)


def render(flags, tf_color, tf_opacity, volume):
    rows = volume.shape[1]
    out = jax.ShapeDtypeStruct((4, rows, LANES), F32)
    vmem = pl.BlockSpec(memory_space=pltpu.VMEM)
    return pl.pallas_call(
        render_kernel,
        in_specs=[pl.BlockSpec(memory_space=pltpu.SMEM), vmem, vmem, vmem],
        out_specs=[vmem, vmem, vmem],
        out_shape=[out, out, jax.ShapeDtypeStruct((2, 8, 8, LANES), F32)],
        scratch_shapes=[pltpu.VMEM((8, LANES), F32)],
        cost_estimate=pl.CostEstimate(flops=40_000_000, bytes_accessed=2_400_000, transcendentals=0),
        compiler_params=pltpu.CompilerParams(vmem_limit_bytes=32 * 1024 * 1024),
        name="render",
    )(flags, tf_color, tf_opacity, volume)


def rim_image(column_ref, rim_ref, flag_ref, tables, rows):
    pairs = BZ * rows // LANES
    bricks = column_ref.shape[0] // pairs
    lane = lane_ids(bricks)
    second = lane >= rows
    deep = lax.broadcasted_iota(jnp.int32, (bricks, LANES), 0)
    flags = jnp.zeros((bricks, LANES), F32)
    for b in range(bricks):
        flags = jnp.where(deep == b, flag_ref[b].astype(F32), flags)
    image = [jnp.zeros((bricks, LANES), F32) for c in range(4)]
    clear = jnp.ones((bricks, LANES), F32)
    for pair in range(pairs):
        f = jnp.where(second, (2 * pair + 1) / BZ, 2 * pair / BZ)
        *own, alpha, fade = classify(column_ref[pl.ds(pair, bricks, stride=pairs), :], tables)
        *left, beside, side_fade = classify(rim_ref[pl.ds(pair, bricks, stride=pairs), :], tables)
        kept = (1.0 - f) * (alpha * fade)
        moved = f * (beside * side_fade)
        sample = [kept * fade * a + moved * side_fade * b for a, b in zip(own, left)] + [kept + moved]
        for part in (sample, [pltpu.roll(value, rows, 1) for value in sample]):
            image = [total + clear * value for total, value in zip(image, part)]
            clear = clear - clear * part[3]
    return [value * flags for value in image]


def deal_kernel(layers, flag_ref, table_ref, opacity_ref, column_ref, rim_ref, run_ref, done_ref, out_ref):
    tables = read_tables(table_ref)
    step = code_step(opacity_ref[...], layers)
    rows = run_ref.shape[1]
    half = rows // 2
    lane = lane_ids(GROUP)
    to_alpha = lane % half + 3 * half
    rim = rim_image(column_ref, rim_ref, flag_ref, tables, rows)
    pieces = LANES // GROUP + 1
    near, far, image = [], [], []
    begun = lane_ids(half) < layers // BZ - 1
    for parity in range(2):
        spread = [pick(value, lane % half * 2 + parity) for value in rim]
        image.append(jnp.where(lane < half, spread[0], jnp.where(
            lane < 2 * half, spread[1], jnp.where(lane < 3 * half, spread[2], spread[3]))))
        place = pl.ds(parity, half, stride=2)
        run = [run_ref[n, place, :] for n in range(3)] + [1.0 - run_ref[3, place, :]]
        done = [done_ref[n, place, :] for n in range(3)] + [1.0 - done_ref[3, place, :]]
        near.append(jnp.concatenate([jnp.where(begun, d, r) for d, r in zip(done, run)], axis=0).T)
        far.append(jnp.concatenate([jnp.where(begun, r, 0.0) for r in run], axis=0).T)
    for m in range(pieces):
        pair = [n[m * GROUP:(m + 1) * GROUP] if m < pieces - 1 else f[:GROUP] for n, f in zip(near, far)]
        if m == 0:
            pair = [piece + (1.0 - pick(piece, to_alpha)) * late for piece, late in zip(pair, image)]
        out_ref[pl.ds(m, GROUP, stride=pieces), :] = pack(*pair, step)


def deal(layers, flags, tables, tf_opacity, column, rim, running, finished):
    vmem = pl.BlockSpec(memory_space=pltpu.VMEM)
    return pl.pallas_call(
        functools.partial(deal_kernel, layers),
        in_specs=[pl.BlockSpec(memory_space=pltpu.SMEM)] + [vmem] * 6,
        out_specs=vmem,
        out_shape=jax.ShapeDtypeStruct((LANES + GROUP, LANES), jnp.int32),
        compiler_params=pltpu.CompilerParams(vmem_limit_bytes=32 * 1024 * 1024),
        name="deal",
    )(flags, tables, tf_opacity, column, rim, running, finished)


def along_depth_kernel(across, down, depth, layers, opacity_ref, arrived_ref, out_ref, total_ref, clear_ref):
    taken = arrived_ref.shape[0] // depth
    step = code_step(opacity_ref[...], layers)
    total_ref[...] = jnp.zeros_like(total_ref)
    clear_ref[...] = jnp.ones_like(clear_ref)
    quarter = LANES // 4
    lane = lane_ids(taken)
    to_alpha = lane % quarter + 3 * quarter
    for z in range(depth):
        place = slice(z, z + taken)
        for parity, piece in enumerate(unpack(arrived_ref[z * taken:(z + 1) * taken, :], step)):
            alpha = pick(piece, to_alpha)
            clear = clear_ref[parity, place, :]
            total_ref[parity, place, :] = total_ref[parity, place, :] + clear * piece
            clear_ref[parity, place, :] = clear - clear * alpha
    blocks = [[total_ref[parity, q * down:(q + 1) * down, :] for q in range(3)] for parity in range(2)]
    empty = jnp.zeros((down, LANES), F32)
    even, odd = blocks[0] + [empty], blocks[1] + [empty]
    step = code_step(opacity_ref[...], layers * depth)
    x = lax.axis_index("gx")
    for q in range(across):
        place = lax.rem(x + q, across) * down
        out_ref[pl.ds(pl.multiple_of(place, down), down), :] = pack(even[q], odd[(q + 2) % 4], step)


def along_depth(layers, tf_opacity, arrived, across, down, depth):
    return pl.pallas_call(
        functools.partial(along_depth_kernel, across, down, depth, layers),
        out_shape=jax.ShapeDtypeStruct((across * down, LANES), jnp.int32),
        scratch_shapes=[pltpu.VMEM((2, 3 * down, LANES), F32), pltpu.VMEM((2, 3 * down, LANES), F32)],
        compiler_params=pltpu.CompilerParams(vmem_limit_bytes=32 * 1024 * 1024),
        name="along_depth",
    )(tf_opacity, arrived)


def gather_kernel(across, down, layers, opacity_ref, arrived_ref, out_ref):
    step = code_step(opacity_ref[...], layers)
    me = lax.axis_index("gx")
    half = LANES // 4
    lane = lane_ids(down)
    to_alpha = lane % half + 3 * half
    total = [jnp.zeros((down, LANES), F32) for k in range(3)]
    clear = [jnp.ones((down, LANES), F32) for k in range(3)]
    for x in reversed(range(across)):
        slots = (jnp.where(me < x, 1, 0), jnp.where(me >= x + 2, 1, 2))
        for parity, piece in enumerate(unpack(arrived_ref[x * down:(x + 1) * down, :], step)):
            alpha = pick(piece, to_alpha)
            for k in range(2) if parity == 0 else range(1, 3):
                mine = jnp.where(slots[parity] == k, 1.0, 0.0)
                total[k] = total[k] + clear[k] * (piece * mine)
                clear[k] = clear[k] - clear[k] * (alpha * mine)
    width = 3 * half
    third = lane % 3
    for c in range(4):
        source = jnp.minimum(lane // 3, half - 1) + c * half
        spread = [pick(value, source) for value in total]
        row = jnp.where(third == 0, spread[0], jnp.where(third == 1, spread[1], spread[2]))
        for y in range(down):
            out_ref[c, 0:1, y * width:(y + 1) * width] = row[y:y + 1, 0:width]


def gather(layers, tf_opacity, arrived, across, down):
    pixels = down * 3 * LANES // 4
    return pl.pallas_call(
        functools.partial(gather_kernel, across, down, layers),
        out_shape=jax.ShapeDtypeStruct((4, 1, pixels), F32),
        compiler_params=pltpu.CompilerParams(vmem_limit_bytes=32 * 1024 * 1024),
        name="gather",
    )(tf_opacity, arrived)


def ends_kernel(volume_ref, first_ref, last_ref):
    layers, rows, cols = volume_ref.shape
    part = 16
    row = lax.broadcasted_iota(jnp.int32, (16, cols), 0)
    lane = lax.broadcasted_iota(jnp.int32, (16, cols), 1)
    unit = jnp.where(lane == jnp.where(row == 0, 0, cols - 1), 1.0, 0.0).astype(jnp.bfloat16)
    for start in range(0, layers, part):
        cells = volume_ref[start:start + part].reshape(part * rows, cols)
        both = lax.dot_general(unit, cells, (((1,), (1,)), ((), ())), preferred_element_type=F32)
        first_ref[:, start * rows:(start + part) * rows] = both[0:1]
        last_ref[:, start * rows:(start + part) * rows] = both[1:2]


def ends(volume):
    layers, rows, cols = volume.shape
    out = jax.ShapeDtypeStruct((1, layers * rows), F32)
    first, last = pl.pallas_call(
        ends_kernel,
        out_shape=[out, out],
        compiler_params=pltpu.CompilerParams(vmem_limit_bytes=32 * 1024 * 1024),
        name="ends",
    )(volume)
    return first.reshape(-1, LANES), last.reshape(-1, LANES)


def body(volume, tf_color, tf_opacity, active):
    layers = volume.shape[0]
    bricks = layers // BZ
    across, down, depth = (lax.axis_size(name) for name in ("gx", "gy", "gz"))
    opacity = tf_opacity.reshape(1, -1)
    flags = active.reshape(bricks)
    column, last = ends(volume)
    rim = lax.ppermute(last, "gx", [(i, i + 1) for i in range(across - 1)])
    running, finished, tables = render(flags, tf_color, opacity, volume)
    rows = deal(layers, flags, tables, opacity, column, rim, running, finished)
    swapped = lax.all_to_all(rows.reshape(depth, 1, -1), "gz", 0, 0, tiled=True)
    merged = along_depth(layers, opacity, swapped.reshape(-1, LANES), across, down, depth)
    arrived = lax.all_to_all(merged.reshape(across * down, 1, -1), ("gx", "gy"), 0, 0, tiled=True)
    return gather(layers * depth, opacity, arrived.reshape(-1, LANES), across, down)


def solution(mesh):
    placed = (P("gz", "gy", "gx"), P(), P(), P("gz", "gy", "gx"))
    return jax.shard_map(
        body,
        mesh=mesh,
        in_specs=placed,
        out_specs=P(None, ("gx", "gy", "gz"), None),
        check_vma=False,
    )
```

```python
import functools

import jax
import jax.numpy as jnp
from jax import lax
from jax.experimental import pallas as pl
from jax.experimental.pallas import tpu as pltpu
from jax.sharding import PartitionSpec as P

BZ = 8
LIMIT = 3.0
KNOTS = 16
LANES = 128
GROUP = 16
STRIP = 32
F32 = jnp.float32


def lane_ids(rows):
    return lax.broadcasted_iota(jnp.int32, (rows, LANES), 1)


def pick(table, index):
    return jnp.take_along_axis(table, index, axis=1, mode="promise_in_bounds")


def code_step(opacity, layers):
    clear = 1.0 - jnp.max(opacity, axis=1, keepdims=True)
    left = jnp.ones_like(clear)
    while layers:
        if layers % 2:
            left = left * clear
        clear = clear * clear
        layers //= 2
    return (1.0 - left) * (1.0 / 65500.0)


def pack(even, odd, step):
    per = 1.0 / step
    low = (even * per + 0.5).astype(jnp.int32)
    high = (odd * per + 0.5).astype(jnp.int32)
    return lax.shift_left(high, 16) | low


def unpack(word, step):
    low = (word & 0xFFFF).astype(F32) * step
    high = lax.shift_right_logical(word, 16).astype(F32) * step
    return low, high


def build_tables(color_ref, opacity_ref, pad_ref, table_ref):
    pad_ref[...] = jnp.zeros_like(pad_ref)
    pad_ref[0:3, 0:KNOTS] = color_ref[...]
    pad_ref[3:4, 0:KNOTS] = opacity_ref[...]
    knots = pad_ref[...]
    lane = lane_ids(8)
    rise = pltpu.roll(knots, LANES - 1, 1) - knots
    bend = jnp.where(lane < KNOTS - 2, pltpu.roll(rise, LANES - 1, 1) - rise, 0.0)
    row = lax.broadcasted_iota(jnp.int32, (8, LANES), 0)
    for m, source in enumerate((2.0 * knots, 4.0 * rise, 4.0 * bend)):
        for n in range(4):
            table_ref[m * 4 + n] = pick(jnp.broadcast_to(source[n:n + 1], (8, LANES)), 2 * row)


def read_tables(table_ref):
    return [table_ref[n] for n in range(12)]


def classify(values, tables):
    scale = 0.5 * (KNOTS - 1) / (2.0 * LIMIT)
    parts = []
    for start in range(0, values.shape[0], 8):
        along = values[start:start + 8] * scale + LIMIT * scale
        place = jnp.clip(along, 0.0, 0.5 * (KNOTS - 1))
        fade = jnp.maximum(0.5 - jnp.abs(along - place), 0.0)
        index = place.astype(jnp.int32)
        place = place - index.astype(F32)
        past = jnp.maximum(place - 0.5, 0.0)
        base, slope, bend = [[take(table, index) for table in tables[m:m + 4]] for m in (0, 4, 8)]
        parts.append([base[n] + slope[n] * place + bend[n] * past for n in range(4)] + [fade])
    return [jnp.concatenate(part, axis=0) for part in zip(*parts)]


def take(table, index):
    return jnp.take_along_axis(table, index, axis=0, mode="promise_in_bounds")


def render_kernel(flag_ref, color_ref, opacity_ref, volume_ref, run_ref, done_ref, table_ref, pad_ref):
    rows_all = run_ref.shape[1]
    groups = rows_all // STRIP
    bricks = volume_ref.shape[0] // BZ

    build_tables(color_ref, opacity_ref, pad_ref, table_ref)
    for ref in (run_ref, done_ref):
        ref[0:3] = jnp.zeros((3, rows_all, LANES), F32)
        ref[3] = jnp.ones((rows_all, LANES), F32)

    lane = lane_ids(STRIP)

    def group_of(brick, rows):
        tables = read_tables(table_ref)
        for k in range(BZ):
            f = k / BZ
            *shades, alpha, fade = classify(volume_ref[brick * BZ + k, rows, :].astype(F32), tables)
            alpha = alpha * fade
            if k == 0:
                weight = alpha * fade
                here = [weight * shade for shade in shades]
                clear = 1.0 - alpha
                continue
            moved = alpha * f
            kept = alpha - moved
            weight = clear * kept * fade
            beside = pltpu.roll(clear, LANES - 1, 1) * moved * fade
            here = [h + weight * shade for h, shade in zip(here, shades)]
            if k == 1:
                right = [beside * shade for shade in shades]
            else:
                right = [r + beside * shade for r, shade in zip(right, shades)]
            clear = clear - clear * (kept + pltpu.roll(moved, 1, 1))
        shown = jnp.where(lane == 0, 0.0, 1.0)
        passed = jnp.where(lane == LANES - 1, 0.0, 1.0)
        image = [pltpu.roll(h * shown, brick, 1) + pltpu.roll(r * passed, brick + 1, 1)
                 for h, r in zip(here, right)]
        image.append(pltpu.roll((1.0 - clear) * shown, brick, 1))
        through = run_ref[3, rows, :]
        for n in range(3):
            run_ref[n, rows, :] = run_ref[n, rows, :] + through * image[n]
        run_ref[3, rows, :] = through - through * image[3]

    def leave(first, last):
        leaving = (lane >= first) & (lane < last)
        for group in range(groups):
            rows = slice(group * STRIP, (group + 1) * STRIP)
            for n in range(4):
                value = run_ref[n, rows, :]
                done_ref[n, rows, :] = jnp.where(leaving, value, done_ref[n, rows, :])
                run_ref[n, rows, :] = jnp.where(leaving, float(n == 3), value)

    def one(brick, left):
        active = flag_ref[brick] > 0

        @pl.when(active)
        def _():
            leave(left, brick)
            for group in range(groups):
                group_of(brick, slice(group * STRIP, (group + 1) * STRIP))

        return jnp.where(active, brick, left)

    leave(lax.fori_loop(0, bricks, one, 0), bricks - 1)


def render(flags, tf_color, tf_opacity, volume):
    rows = volume.shape[1]
    out = jax.ShapeDtypeStruct((4, rows, LANES), F32)
    vmem = pl.BlockSpec(memory_space=pltpu.VMEM)
    return pl.pallas_call(
        render_kernel,
        in_specs=[pl.BlockSpec(memory_space=pltpu.SMEM), vmem, vmem, vmem],
        out_specs=[vmem, vmem, vmem],
        out_shape=[out, out, jax.ShapeDtypeStruct((12, 8, LANES), F32)],
        scratch_shapes=[pltpu.VMEM((8, LANES), F32)],
        cost_estimate=pl.CostEstimate(flops=40_000_000, bytes_accessed=2_400_000, transcendentals=0),
        compiler_params=pltpu.CompilerParams(vmem_limit_bytes=32 * 1024 * 1024),
        name="render",
    )(flags, tf_color, tf_opacity, volume)


def rim_image(column_ref, rim_ref, flag_ref, tables, rows):
    pairs = BZ * rows // LANES
    bricks = column_ref.shape[0] // pairs
    lane = lane_ids(bricks)
    second = lane >= rows
    deep = lax.broadcasted_iota(jnp.int32, (bricks, LANES), 0)
    flags = jnp.zeros((bricks, LANES), F32)
    for b in range(bricks):
        flags = jnp.where(deep == b, flag_ref[b].astype(F32), flags)
    image = [jnp.zeros((bricks, LANES), F32) for c in range(4)]
    clear = jnp.ones((bricks, LANES), F32)
    for pair in range(pairs):
        f = jnp.where(second, (2 * pair + 1) / BZ, 2 * pair / BZ)
        *own, alpha, fade = classify(column_ref[pl.ds(pair, bricks, stride=pairs), :], tables)
        *left, beside, side_fade = classify(rim_ref[pl.ds(pair, bricks, stride=pairs), :], tables)
        kept = (1.0 - f) * (alpha * fade)
        moved = f * (beside * side_fade)
        sample = [kept * fade * a + moved * side_fade * b for a, b in zip(own, left)] + [kept + moved]
        for part in (sample, [pltpu.roll(value, rows, 1) for value in sample]):
            image = [total + clear * value for total, value in zip(image, part)]
            clear = clear - clear * part[3]
    return [value * flags for value in image]


def deal_kernel(layers, flag_ref, table_ref, opacity_ref, column_ref, rim_ref, run_ref, done_ref, out_ref):
    tables = read_tables(table_ref)
    step = code_step(opacity_ref[...], layers)
    rows = run_ref.shape[1]
    half = rows // 2
    lane = lane_ids(GROUP)
    to_alpha = lane % half + 3 * half
    rim = rim_image(column_ref, rim_ref, flag_ref, tables, rows)
    pieces = LANES // GROUP + 1
    near, far, image = [], [], []
    begun = lane_ids(half) < layers // BZ - 1
    for parity in range(2):
        spread = [pick(value, lane % half * 2 + parity) for value in rim]
        image.append(jnp.where(lane < half, spread[0], jnp.where(
            lane < 2 * half, spread[1], jnp.where(lane < 3 * half, spread[2], spread[3]))))
        place = pl.ds(parity, half, stride=2)
        run = [run_ref[n, place, :] for n in range(3)] + [1.0 - run_ref[3, place, :]]
        done = [done_ref[n, place, :] for n in range(3)] + [1.0 - done_ref[3, place, :]]
        near.append(jnp.concatenate([jnp.where(begun, d, r) for d, r in zip(done, run)], axis=0).T)
        far.append(jnp.concatenate([jnp.where(begun, r, 0.0) for r in run], axis=0).T)
    for m in range(pieces):
        pair = [n[m * GROUP:(m + 1) * GROUP] if m < pieces - 1 else f[:GROUP] for n, f in zip(near, far)]
        if m == 0:
            pair = [piece + (1.0 - pick(piece, to_alpha)) * late for piece, late in zip(pair, image)]
        out_ref[pl.ds(m, GROUP, stride=pieces), :] = pack(*pair, step)


def deal(layers, flags, tables, tf_opacity, column, rim, running, finished):
    vmem = pl.BlockSpec(memory_space=pltpu.VMEM)
    return pl.pallas_call(
        functools.partial(deal_kernel, layers),
        in_specs=[pl.BlockSpec(memory_space=pltpu.SMEM)] + [vmem] * 6,
        out_specs=vmem,
        out_shape=jax.ShapeDtypeStruct((LANES + GROUP, LANES), jnp.int32),
        compiler_params=pltpu.CompilerParams(vmem_limit_bytes=32 * 1024 * 1024),
        name="deal",
    )(flags, tables, tf_opacity, column, rim, running, finished)


def along_depth_kernel(across, down, depth, layers, opacity_ref, arrived_ref, out_ref, total_ref, clear_ref):
    taken = arrived_ref.shape[0] // depth
    step = code_step(opacity_ref[...], layers)
    total_ref[...] = jnp.zeros_like(total_ref)
    clear_ref[...] = jnp.ones_like(clear_ref)
    quarter = LANES // 4
    lane = lane_ids(taken)
    to_alpha = lane % quarter + 3 * quarter
    for z in range(depth):
        place = slice(z, z + taken)
        for parity, piece in enumerate(unpack(arrived_ref[z * taken:(z + 1) * taken, :], step)):
            alpha = pick(piece, to_alpha)
            clear = clear_ref[parity, place, :]
            total_ref[parity, place, :] = total_ref[parity, place, :] + clear * piece
            clear_ref[parity, place, :] = clear - clear * alpha
    blocks = [[total_ref[parity, q * down:(q + 1) * down, :] for q in range(3)] for parity in range(2)]
    empty = jnp.zeros((down, LANES), F32)
    even, odd = blocks[0] + [empty], blocks[1] + [empty]
    step = code_step(opacity_ref[...], layers * depth)
    x = lax.axis_index("gx")
    for q in range(across):
        place = lax.rem(x + q, across) * down
        out_ref[pl.ds(pl.multiple_of(place, down), down), :] = pack(even[q], odd[(q + 2) % 4], step)


def along_depth(layers, tf_opacity, arrived, across, down, depth):
    return pl.pallas_call(
        functools.partial(along_depth_kernel, across, down, depth, layers),
        out_shape=jax.ShapeDtypeStruct((across * down, LANES), jnp.int32),
        scratch_shapes=[pltpu.VMEM((2, 3 * down, LANES), F32), pltpu.VMEM((2, 3 * down, LANES), F32)],
        compiler_params=pltpu.CompilerParams(vmem_limit_bytes=32 * 1024 * 1024),
        name="along_depth",
    )(tf_opacity, arrived)


def gather_kernel(across, down, layers, opacity_ref, arrived_ref, out_ref):
    step = code_step(opacity_ref[...], layers)
    me = lax.axis_index("gx")
    half = LANES // 4
    lane = lane_ids(down)
    to_alpha = lane % half + 3 * half
    total = [jnp.zeros((down, LANES), F32) for k in range(3)]
    clear = [jnp.ones((down, LANES), F32) for k in range(3)]
    for x in reversed(range(across)):
        slots = (jnp.where(me < x, 1, 0), jnp.where(me >= x + 2, 1, 2))
        for parity, piece in enumerate(unpack(arrived_ref[x * down:(x + 1) * down, :], step)):
            alpha = pick(piece, to_alpha)
            for k in range(2) if parity == 0 else range(1, 3):
                mine = jnp.where(slots[parity] == k, 1.0, 0.0)
                total[k] = total[k] + clear[k] * (piece * mine)
                clear[k] = clear[k] - clear[k] * (alpha * mine)
    width = 3 * half
    third = lane % 3
    for c in range(4):
        source = jnp.minimum(lane // 3, half - 1) + c * half
        spread = [pick(value, source) for value in total]
        row = jnp.where(third == 0, spread[0], jnp.where(third == 1, spread[1], spread[2]))
        for y in range(down):
            out_ref[c, 0:1, y * width:(y + 1) * width] = row[y:y + 1, 0:width]


def gather(layers, tf_opacity, arrived, across, down):
    pixels = down * 3 * LANES // 4
    return pl.pallas_call(
        functools.partial(gather_kernel, across, down, layers),
        out_shape=jax.ShapeDtypeStruct((4, 1, pixels), F32),
        compiler_params=pltpu.CompilerParams(vmem_limit_bytes=32 * 1024 * 1024),
        name="gather",
    )(tf_opacity, arrived)


def ends_kernel(volume_ref, first_ref, last_ref):
    layers, rows, cols = volume_ref.shape
    part = 16
    row = lax.broadcasted_iota(jnp.int32, (16, cols), 0)
    lane = lax.broadcasted_iota(jnp.int32, (16, cols), 1)
    unit = jnp.where(lane == jnp.where(row == 0, 0, cols - 1), 1.0, 0.0).astype(jnp.bfloat16)
    for start in range(0, layers, part):
        cells = volume_ref[start:start + part].reshape(part * rows, cols)
        both = lax.dot_general(unit, cells, (((1,), (1,)), ((), ())), preferred_element_type=F32)
        first_ref[:, start * rows:(start + part) * rows] = both[0:1]
        last_ref[:, start * rows:(start + part) * rows] = both[1:2]


def ends(volume):
    layers, rows, cols = volume.shape
    out = jax.ShapeDtypeStruct((1, layers * rows), F32)
    first, last = pl.pallas_call(
        ends_kernel,
        out_shape=[out, out],
        compiler_params=pltpu.CompilerParams(vmem_limit_bytes=32 * 1024 * 1024),
        name="ends",
    )(volume)
    return first.reshape(-1, LANES), last.reshape(-1, LANES)


def body(volume, tf_color, tf_opacity, active):
    layers = volume.shape[0]
    bricks = layers // BZ
    across, down, depth = (lax.axis_size(name) for name in ("gx", "gy", "gz"))
    opacity = tf_opacity.reshape(1, -1)
    flags = active.reshape(bricks)
    column, last = ends(volume)
    rim = lax.ppermute(last, "gx", [(i, i + 1) for i in range(across - 1)])
    running, finished, tables = render(flags, tf_color, opacity, volume)
    rows = deal(layers, flags, tables, opacity, column, rim, running, finished)
    swapped = lax.all_to_all(rows.reshape(depth, 1, -1), "gz", 0, 0, tiled=True)
    merged = along_depth(layers, opacity, swapped.reshape(-1, LANES), across, down, depth)
    arrived = lax.all_to_all(merged.reshape(across * down, 1, -1), ("gx", "gy"), 0, 0, tiled=True)
    return gather(layers * depth, opacity, arrived.reshape(-1, LANES), across, down)


def solution(mesh):
    placed = (P("gz", "gy", "gx"), P(), P(), P("gz", "gy", "gx"))
    return jax.shard_map(
        body,
        mesh=mesh,
        in_specs=placed,
        out_specs=P(None, ("gx", "gy", "gz"), None),
        check_vma=False,
    )
```

```python
import functools

import jax
import jax.numpy as jnp
from jax import lax
from jax.experimental import pallas as pl
from jax.experimental.pallas import tpu as pltpu
from jax.sharding import PartitionSpec as P

BZ = 8
LIMIT = 3.0
KNOTS = 16
LANES = 128
GROUP = 16
STRIP = 32
F32 = jnp.float32


def lane_ids(rows):
    return lax.broadcasted_iota(jnp.int32, (rows, LANES), 1)


def pick(table, index):
    return jnp.take_along_axis(table, index, axis=1, mode="promise_in_bounds")


def code_step(opacity, layers):
    clear = 1.0 - jnp.max(opacity, axis=1, keepdims=True)
    left = jnp.ones_like(clear)
    while layers:
        if layers % 2:
            left = left * clear
        clear = clear * clear
        layers //= 2
    return (1.0 - left) * (1.0 / 65500.0)


def pack(even, odd, step):
    per = 1.0 / step
    low = (even * per + 0.5).astype(jnp.int32)
    high = (odd * per + 0.5).astype(jnp.int32)
    return lax.shift_left(high, 16) | low


def unpack(word, step):
    low = (word & 0xFFFF).astype(F32) * step
    high = lax.shift_right_logical(word, 16).astype(F32) * step
    return low, high


def build_tables(color_ref, opacity_ref, pad_ref, table_ref):
    pad_ref[...] = jnp.zeros_like(pad_ref)
    pad_ref[0:3, 0:KNOTS] = color_ref[...]
    pad_ref[3:4, 0:KNOTS] = opacity_ref[...]
    knots = pad_ref[...]
    lane = lane_ids(8)
    rise = pltpu.roll(knots, LANES - 1, 1) - knots
    bend = jnp.where(lane < KNOTS - 2, pltpu.roll(rise, LANES - 1, 1) - rise, 0.0)
    row = lax.broadcasted_iota(jnp.int32, (8, LANES), 0)
    for m, source in enumerate((2.0 * knots, 4.0 * rise, 4.0 * bend)):
        for n in range(4):
            table_ref[m * 4 + n] = pick(jnp.broadcast_to(source[n:n + 1], (8, LANES)), 2 * row)


def read_tables(table_ref):
    return [table_ref[n] for n in range(12)]


def classify(values, tables):
    scale = 0.5 * (KNOTS - 1) / (2.0 * LIMIT)
    parts = []
    for start in range(0, values.shape[0], 8):
        along = values[start:start + 8] * scale + LIMIT * scale
        place = jnp.clip(along, 0.0, 0.5 * (KNOTS - 1))
        fade = jnp.maximum(0.5 - jnp.abs(along - place), 0.0)
        index = place.astype(jnp.int32)
        place = place - index.astype(F32)
        past = jnp.maximum(place - 0.5, 0.0)
        base, slope, bend = [[take(table, index) for table in tables[m:m + 4]] for m in (0, 4, 8)]
        parts.append([base[n] + slope[n] * place + bend[n] * past for n in range(4)] + [fade])
    return [jnp.concatenate(part, axis=0) for part in zip(*parts)]


def take(table, index):
    return jnp.take_along_axis(table, index, axis=0, mode="promise_in_bounds")


def render_kernel(flag_ref, color_ref, opacity_ref, volume_ref, run_ref, done_ref, table_ref, pad_ref):
    rows_all = run_ref.shape[1]
    groups = rows_all // STRIP
    bricks = volume_ref.shape[0] // BZ

    build_tables(color_ref, opacity_ref, pad_ref, table_ref)
    for ref in (run_ref, done_ref):
        ref[0:3] = jnp.zeros((3, rows_all, LANES), F32)
        ref[3] = jnp.ones((rows_all, LANES), F32)

    lane = lane_ids(STRIP)

    def group_of(brick, rows):
        tables = read_tables(table_ref)
        for k in range(BZ):
            f = k / BZ
            *shades, alpha, fade = classify(volume_ref[brick * BZ + k, rows, :].astype(F32), tables)
            alpha = alpha * fade
            if k == 0:
                weight = alpha * fade
                here = [weight * shade for shade in shades]
                clear = 1.0 - alpha
                continue
            moved = alpha * f
            kept = alpha - moved
            weight = clear * kept * fade
            beside = pltpu.roll(clear, LANES - 1, 1) * moved * fade
            here = [h + weight * shade for h, shade in zip(here, shades)]
            if k == 1:
                right = [beside * shade for shade in shades]
            else:
                right = [r + beside * shade for r, shade in zip(right, shades)]
            clear = clear - clear * (kept + pltpu.roll(moved, 1, 1))
        through = run_ref[3, rows, :]
        open_here = jnp.where(lane == brick, 0.0, through)
        for n in range(3):
            image = pltpu.roll(here[n], brick, 1) + pltpu.roll(right[n], brick + 1, 1)
            run_ref[n, rows, :] = run_ref[n, rows, :] + open_here * image
        run_ref[3, rows, :] = through - open_here * (1.0 - pltpu.roll(clear, brick, 1))

    def leave(first, last):
        leaving = (lane >= first) & (lane < last)
        for group in range(groups):
            rows = slice(group * STRIP, (group + 1) * STRIP)
            for n in range(4):
                value = run_ref[n, rows, :]
                done_ref[n, rows, :] = jnp.where(leaving, value, done_ref[n, rows, :])
                run_ref[n, rows, :] = jnp.where(leaving, float(n == 3), value)

    def one(brick, left):
        active = flag_ref[brick] > 0

        @pl.when(active)
        def _():
            leave(left, brick)
            for group in range(groups):
                group_of(brick, slice(group * STRIP, (group + 1) * STRIP))

        return jnp.where(active, brick, left)

    leave(lax.fori_loop(0, bricks, one, 0), bricks - 1)


def render(flags, tf_color, tf_opacity, volume):
    rows = volume.shape[1]
    out = jax.ShapeDtypeStruct((4, rows, LANES), F32)
    vmem = pl.BlockSpec(memory_space=pltpu.VMEM)
    return pl.pallas_call(
        render_kernel,
        in_specs=[pl.BlockSpec(memory_space=pltpu.SMEM), vmem, vmem, vmem],
        out_specs=[vmem, vmem, vmem],
        out_shape=[out, out, jax.ShapeDtypeStruct((12, 8, LANES), F32)],
        scratch_shapes=[pltpu.VMEM((8, LANES), F32)],
        cost_estimate=pl.CostEstimate(flops=40_000_000, bytes_accessed=2_400_000, transcendentals=0),
        compiler_params=pltpu.CompilerParams(vmem_limit_bytes=32 * 1024 * 1024),
        name="render",
    )(flags, tf_color, tf_opacity, volume)


def rim_image(column_ref, rim_ref, flag_ref, tables, rows):
    pairs = BZ * rows // LANES
    bricks = column_ref.shape[0] // pairs
    lane = lane_ids(bricks)
    second = lane >= rows
    deep = lax.broadcasted_iota(jnp.int32, (bricks, LANES), 0)
    flags = jnp.zeros((bricks, LANES), F32)
    for b in range(bricks):
        flags = jnp.where(deep == b, flag_ref[b].astype(F32), flags)
    image = [jnp.zeros((bricks, LANES), F32) for c in range(4)]
    clear = jnp.ones((bricks, LANES), F32)
    for pair in range(pairs):
        f = jnp.where(second, (2 * pair + 1) / BZ, 2 * pair / BZ)
        *own, alpha, fade = classify(column_ref[pl.ds(pair, bricks, stride=pairs), :], tables)
        *left, beside, side_fade = classify(rim_ref[pl.ds(pair, bricks, stride=pairs), :], tables)
        kept = (1.0 - f) * (alpha * fade)
        moved = f * (beside * side_fade)
        sample = [kept * fade * a + moved * side_fade * b for a, b in zip(own, left)] + [kept + moved]
        for part in (sample, [pltpu.roll(value, rows, 1) for value in sample]):
            image = [total + clear * value for total, value in zip(image, part)]
            clear = clear - clear * part[3]
    return [value * flags for value in image]


def deal_kernel(layers, flag_ref, table_ref, opacity_ref, column_ref, rim_ref, run_ref, done_ref, out_ref):
    tables = read_tables(table_ref)
    step = code_step(opacity_ref[...], layers)
    rows = run_ref.shape[1]
    half = rows // 2
    lane = lane_ids(GROUP)
    to_alpha = lane % half + 3 * half
    rim = rim_image(column_ref, rim_ref, flag_ref, tables, rows)
    pieces = LANES // GROUP + 1
    near, far, image = [], [], []
    begun = lane_ids(half) < layers // BZ - 1
    for parity in range(2):
        spread = [pick(value, lane % half * 2 + parity) for value in rim]
        image.append(jnp.where(lane < half, spread[0], jnp.where(
            lane < 2 * half, spread[1], jnp.where(lane < 3 * half, spread[2], spread[3]))))
        place = pl.ds(parity, half, stride=2)
        run = [run_ref[n, place, :] for n in range(3)] + [1.0 - run_ref[3, place, :]]
        done = [done_ref[n, place, :] for n in range(3)] + [1.0 - done_ref[3, place, :]]
        near.append(jnp.concatenate([jnp.where(begun, d, r) for d, r in zip(done, run)], axis=0).T)
        far.append(jnp.concatenate([jnp.where(begun, r, 0.0) for r in run], axis=0).T)
    for m in range(pieces):
        pair = [n[m * GROUP:(m + 1) * GROUP] if m < pieces - 1 else f[:GROUP] for n, f in zip(near, far)]
        if m == 0:
            pair = [piece + (1.0 - pick(piece, to_alpha)) * late for piece, late in zip(pair, image)]
        out_ref[pl.ds(m, GROUP, stride=pieces), :] = pack(*pair, step)


def deal(layers, flags, tables, tf_opacity, column, rim, running, finished):
    vmem = pl.BlockSpec(memory_space=pltpu.VMEM)
    return pl.pallas_call(
        functools.partial(deal_kernel, layers),
        in_specs=[pl.BlockSpec(memory_space=pltpu.SMEM)] + [vmem] * 6,
        out_specs=vmem,
        out_shape=jax.ShapeDtypeStruct((LANES + GROUP, LANES), jnp.int32),
        compiler_params=pltpu.CompilerParams(vmem_limit_bytes=32 * 1024 * 1024),
        name="deal",
    )(flags, tables, tf_opacity, column, rim, running, finished)


def along_depth_kernel(across, down, depth, layers, opacity_ref, arrived_ref, out_ref, total_ref, clear_ref):
    taken = arrived_ref.shape[0] // depth
    step = code_step(opacity_ref[...], layers)
    total_ref[...] = jnp.zeros_like(total_ref)
    clear_ref[...] = jnp.ones_like(clear_ref)
    quarter = LANES // 4
    lane = lane_ids(taken)
    to_alpha = lane % quarter + 3 * quarter
    for z in range(depth):
        place = slice(z, z + taken)
        for parity, piece in enumerate(unpack(arrived_ref[z * taken:(z + 1) * taken, :], step)):
            alpha = pick(piece, to_alpha)
            clear = clear_ref[parity, place, :]
            total_ref[parity, place, :] = total_ref[parity, place, :] + clear * piece
            clear_ref[parity, place, :] = clear - clear * alpha
    blocks = [[total_ref[parity, q * down:(q + 1) * down, :] for q in range(3)] for parity in range(2)]
    empty = jnp.zeros((down, LANES), F32)
    even, odd = blocks[0] + [empty], blocks[1] + [empty]
    step = code_step(opacity_ref[...], layers * depth)
    x = lax.axis_index("gx")
    for q in range(across):
        place = lax.rem(x + q, across) * down
        out_ref[pl.ds(pl.multiple_of(place, down), down), :] = pack(even[q], odd[(q + 2) % 4], step)


def along_depth(layers, tf_opacity, arrived, across, down, depth):
    return pl.pallas_call(
        functools.partial(along_depth_kernel, across, down, depth, layers),
        out_shape=jax.ShapeDtypeStruct((across * down, LANES), jnp.int32),
        scratch_shapes=[pltpu.VMEM((2, 3 * down, LANES), F32), pltpu.VMEM((2, 3 * down, LANES), F32)],
        compiler_params=pltpu.CompilerParams(vmem_limit_bytes=32 * 1024 * 1024),
        name="along_depth",
    )(tf_opacity, arrived)


def gather_kernel(across, down, layers, opacity_ref, arrived_ref, out_ref):
    step = code_step(opacity_ref[...], layers)
    me = lax.axis_index("gx")
    half = LANES // 4
    lane = lane_ids(down)
    to_alpha = lane % half + 3 * half
    total = [jnp.zeros((down, LANES), F32) for k in range(3)]
    clear = [jnp.ones((down, LANES), F32) for k in range(3)]
    for x in reversed(range(across)):
        slots = (jnp.where(me < x, 1, 0), jnp.where(me >= x + 2, 1, 2))
        for parity, piece in enumerate(unpack(arrived_ref[x * down:(x + 1) * down, :], step)):
            alpha = pick(piece, to_alpha)
            for k in range(2) if parity == 0 else range(1, 3):
                mine = jnp.where(slots[parity] == k, 1.0, 0.0)
                total[k] = total[k] + clear[k] * (piece * mine)
                clear[k] = clear[k] - clear[k] * (alpha * mine)
    width = 3 * half
    third = lane % 3
    for c in range(4):
        source = jnp.minimum(lane // 3, half - 1) + c * half
        spread = [pick(value, source) for value in total]
        row = jnp.where(third == 0, spread[0], jnp.where(third == 1, spread[1], spread[2]))
        for y in range(down):
            out_ref[c, 0:1, y * width:(y + 1) * width] = row[y:y + 1, 0:width]


def gather(layers, tf_opacity, arrived, across, down):
    pixels = down * 3 * LANES // 4
    return pl.pallas_call(
        functools.partial(gather_kernel, across, down, layers),
        out_shape=jax.ShapeDtypeStruct((4, 1, pixels), F32),
        compiler_params=pltpu.CompilerParams(vmem_limit_bytes=32 * 1024 * 1024),
        name="gather",
    )(tf_opacity, arrived)


def ends_kernel(volume_ref, first_ref, last_ref):
    layers, rows, cols = volume_ref.shape
    part = 16
    row = lax.broadcasted_iota(jnp.int32, (16, cols), 0)
    lane = lax.broadcasted_iota(jnp.int32, (16, cols), 1)
    unit = jnp.where(lane == jnp.where(row == 0, 0, cols - 1), 1.0, 0.0).astype(jnp.bfloat16)
    for start in range(0, layers, part):
        cells = volume_ref[start:start + part].reshape(part * rows, cols)
        both = lax.dot_general(unit, cells, (((1,), (1,)), ((), ())), preferred_element_type=F32)
        first_ref[:, start * rows:(start + part) * rows] = both[0:1]
        last_ref[:, start * rows:(start + part) * rows] = both[1:2]


def ends(volume):
    layers, rows, cols = volume.shape
    out = jax.ShapeDtypeStruct((1, layers * rows), F32)
    first, last = pl.pallas_call(
        ends_kernel,
        out_shape=[out, out],
        compiler_params=pltpu.CompilerParams(vmem_limit_bytes=32 * 1024 * 1024),
        name="ends",
    )(volume)
    return first.reshape(-1, LANES), last.reshape(-1, LANES)


def body(volume, tf_color, tf_opacity, active):
    layers = volume.shape[0]
    bricks = layers // BZ
    across, down, depth = (lax.axis_size(name) for name in ("gx", "gy", "gz"))
    opacity = tf_opacity.reshape(1, -1)
    flags = active.reshape(bricks)
    column, last = ends(volume)
    rim = lax.ppermute(last, "gx", [(i, i + 1) for i in range(across - 1)])
    running, finished, tables = render(flags, tf_color, opacity, volume)
    rows = deal(layers, flags, tables, opacity, column, rim, running, finished)
    swapped = lax.all_to_all(rows.reshape(depth, 1, -1), "gz", 0, 0, tiled=True)
    merged = along_depth(layers, opacity, swapped.reshape(-1, LANES), across, down, depth)
    arrived = lax.all_to_all(merged.reshape(across * down, 1, -1), ("gx", "gy"), 0, 0, tiled=True)
    return gather(layers * depth, opacity, arrived.reshape(-1, LANES), across, down)


def solution(mesh):
    placed = (P("gz", "gy", "gx"), P(), P(), P("gz", "gy", "gx"))
    return jax.shard_map(
        body,
        mesh=mesh,
        in_specs=placed,
        out_specs=P(None, ("gx", "gy", "gz"), None),
        check_vma=False,
    )
```
